128 devices in a mesh: tile: 8 (over y_hi, z), phase: 16 (over x, y_lo, core).
Axes of the slice: x: 4, y: 4 (y_hi: 2, y_lo: 2; y = y_hi * 2 + y_lo), z: 4, core: 2. Of those that a mesh axis runs over, the one named last changes fastest.
Arguments:
- latent: bfloat16 [1, 256, 256, 640], P(None, 'tile', 'phase'), may hold values from -6 to 6
- previous: bfloat16 [1, 128, 128, 640], P(None, 'tile', 'phase'), may hold values from -6 to 6
- blend_weight: float32 [256, 256], P('tile', 'phase'), may hold values from 0.2 to 0.8
- skip_weight: float32 [256, 256], P('tile', 'phase'), may hold values from 0.1 to 0.5
- norm_gain: float32 [640], replicated, may hold values from 0.5 to 7, as said below
- w_query: bfloat16 [640, 640], replicated, may hold values from -0.25 to 0.25
- w_key: bfloat16 [640, 640], replicated, may hold values from -0.25 to 0.25
- w_value: bfloat16 [640, 640], replicated, may hold values from -0.25 to 0.25
- w_out: bfloat16 [640, 640], replicated, may hold values from -3.59375 to 3.59375
Outputs:
- result: bfloat16 [1, 256, 256, 640], P(None, 'tile', 'phase')
The draws below stay inside these ranges and needn't reach their ends.
Inputs may be any that keep to these rules, and one draw needn't show every extreme that they name: `norm_gain`: positive gains, one a channel.
All inputs are finite; a program needn't handle non-finite values.
Results may differ from the reference program's by a relative error of at most 0.007.
The reference program's roundings to bfloat16 on the way (of `normed`, `queries`, `dilated` and `mixed_rows`) count: a program that leaves them out, or rounds other values in their place, can miss the bound.
Values may be sent and summed in bfloat16 or wider, within the bound.
A program may use at most 128 MiB of HBM per device.

```python
import jax
import jax.numpy as jnp
from jax import lax

C = 640
HEADS = 10
STRIDE = 4
OV = 16
ROWS_DEV = 32
COLS_DEV = 16
BATCH = 1
HH = 256
WW = 256
N_TILE = 8
N_PHASE = 16


def draw_norm_gain(key, part):
    key = jax.random.fold_in(key, 7)
    return jax.random.uniform(key, (C,), jnp.float32, 0.5, 1.5)


def block_scale(rng, dims, shards, smallest, top_value):
    level, own = 1.0, jax.random.fold_in(rng, 6)
    for axis_at, shards_of in shards:
        draws = jnp.exp(jax.random.uniform(jax.random.fold_in(own, axis_at), (shards_of,), jnp.float32, smallest / len(shards), top_value / len(shards)))
        level = level * jnp.repeat(draws, dims[axis_at] // shards_of).reshape([-1 if axis == axis_at else 1 for axis in range(len(dims))])
    return level


def gaussian(own_key, shape, spread, most, cuts=(), kind=jnp.bfloat16):
    values = spread * jax.random.normal(own_key, shape, jnp.float32)
    if cuts:
        values = values * block_scale(own_key, shape, cuts, -0.22, 0.18)
    return jnp.clip(values, -most, most).astype(kind)


def setup_inputs(seed: int = 0) -> dict:
    key_of = jax.random.split(jax.random.key(seed), 10)
    latent = gaussian(key_of[0], (BATCH, HH, WW, C), 1.0, 6.0, ((1, 8), (2, 16)))
    previous = gaussian(key_of[1], (BATCH, HH // 2, WW // 2, C), 1.0, 6.0, ((1, 8), (2, 16)))
    blend_weight = jnp.clip(0.2 + 0.6 * jax.random.uniform(key_of[2], (HH, WW), jnp.float32) ** block_scale(key_of[2], (HH, WW), ((0, 8), (1, 16)), -0.2, 0.2), 0.2, 0.8)
    skip_weight = jnp.clip(0.1 + 0.4 * jax.random.uniform(key_of[3], (HH, WW), jnp.float32) ** block_scale(key_of[3], (HH, WW), ((0, 8), (1, 16)), -0.2, 0.2), 0.1, 0.5)
    norm_gain = draw_norm_gain(jax.random.fold_in(key_of[9], 71), 0)
    w_query = gaussian(key_of[5], (C, C), C ** -0.5, 0.25)
    w_key = gaussian(key_of[6], (C, C), C ** -0.5, 0.25)
    w_value = gaussian(key_of[7], (C, C), C ** -0.5, 0.25)
    w_out = gaussian(key_of[8], (C, C), 0.6, 3.59375)
    return {"latent": latent, "previous": previous, "blend_weight": blend_weight, "skip_weight": skip_weight, "norm_gain": norm_gain, "w_query": w_query, "w_key": w_key, "w_value": w_value, "w_out": w_out}


def layer_norm(tensor, gain_vector):
    widened = tensor.astype(jnp.float32)
    average = lax.optimization_barrier(jnp.mean(widened, axis=-1, keepdims=True))
    centred = widened - average
    variance = lax.optimization_barrier(jnp.mean(centred * centred, axis=-1, keepdims=True))
    return (centred * lax.rsqrt(variance + 1e-05) * gain_vector).astype(jnp.bfloat16)

def attend(queries, key_rows, value_rows, inside):
    head_size = queries.shape[1] // HEADS
    factor = head_size ** (-0.5)

    def one_head(head_index):
        first_col = head_index * head_size
        query_head = lax.dynamic_slice_in_dim(queries, first_col, head_size, 1)
        key_head = lax.dynamic_slice_in_dim(key_rows, first_col, head_size, 1)
        value_head = lax.dynamic_slice_in_dim(value_rows, first_col, head_size, 1)
        scores = jnp.dot(query_head, key_head.T, preferred_element_type=jnp.float32) * factor
        scores = jnp.where(inside[None, :], scores, -1e+30)
        largest = lax.optimization_barrier(jnp.max(scores, axis=1, keepdims=True))
        raised = jnp.exp(scores - largest)
        weights = (raised / lax.optimization_barrier(jnp.sum(raised, axis=1, keepdims=True))).astype(jnp.bfloat16)
        return jnp.dot(weights, value_head, preferred_element_type=jnp.float32)
    stacked = lax.map(one_head, jnp.arange(HEADS, dtype=jnp.int32))
    return stacked.transpose(1, 0, 2).reshape(queries.shape[0], -1)

def reference(latent, previous, blend_weight, skip_weight, norm_gain, w_query, w_key, w_value, w_out):
    image_count, height, breadth, channels = latent.shape
    normed = layer_norm(latent, norm_gain)
    flat_normed = normed.reshape(-1, channels)
    queries = jnp.dot(flat_normed, w_query, preferred_element_type=jnp.float32).astype(jnp.bfloat16).reshape(latent.shape)
    key_rows = jnp.dot(flat_normed, w_key, preferred_element_type=jnp.float32).astype(jnp.bfloat16).reshape(latent.shape)
    value_rows = jnp.dot(flat_normed, w_value, preferred_element_type=jnp.float32).astype(jnp.bfloat16).reshape(latent.shape)
    margin = ((0, 0), (OV, OV), (OV, OV), (0, 0))
    keys_padded = jnp.pad(key_rows, margin)
    values_padded = jnp.pad(value_rows, margin)
    ext_rows = ROWS_DEV + 2 * OV
    ext_cols = COLS_DEV + 2 * OV

    def tile_attend(tile_index):
        row_first = (tile_index // N_PHASE * ROWS_DEV).astype(jnp.int32)
        col_first = (tile_index % N_PHASE * COLS_DEV).astype(jnp.int32)
        anchor = jnp.zeros((), jnp.int32)
        starts = (anchor, row_first, col_first, anchor)
        tile_query = lax.dynamic_slice(queries, starts, (image_count, ROWS_DEV, COLS_DEV, channels))
        tile_keys = lax.dynamic_slice(keys_padded, starts, (image_count, ext_rows, ext_cols, channels))
        tile_values = lax.dynamic_slice(values_padded, starts, (image_count, ext_rows, ext_cols, channels))
        row_where = row_first - OV + jnp.arange(ext_rows, dtype=jnp.int32)
        col_where = col_first - OV + jnp.arange(ext_cols, dtype=jnp.int32)
        inside = (((row_where >= 0) & (row_where < height))[:, None] & ((col_where >= 0) & (col_where < breadth))[None, :]).reshape(-1)

        def per_image(triple):
            return attend(triple[0].reshape(-1, channels), triple[1].reshape(-1, channels), triple[2].reshape(-1, channels), inside)
        return lax.map(per_image, (tile_query, tile_keys, tile_values))
    tile_outs = lax.map(tile_attend, jnp.arange(N_TILE * N_PHASE, dtype=jnp.int32))
    local_out = tile_outs.reshape(N_TILE, N_PHASE, image_count, ROWS_DEV, COLS_DEV, channels)
    local_out = local_out.transpose(2, 0, 3, 1, 4, 5).reshape(latent.shape)

    def to_phases(tensor):
        split = tensor.reshape(image_count, height // STRIDE, STRIDE, breadth // STRIDE, STRIDE, channels)
        return split.transpose(2, 4, 0, 1, 3, 5).reshape(STRIDE * STRIDE * image_count, -1, channels)
    inside_all = jnp.ones((height * breadth // (STRIDE * STRIDE),), dtype=bool)
    block_rows = ROWS_DEV * COLS_DEV

    def phase_attend(triple):
        blocks = triple[0].reshape(-1, block_rows, channels)

        def per_block(query_block):
            return attend(query_block, triple[1], triple[2], inside_all)
        return lax.map(per_block, blocks).reshape(-1, channels).astype(jnp.bfloat16)
    dilated = lax.map(phase_attend, (to_phases(queries), to_phases(key_rows), to_phases(value_rows)))
    dilated = dilated.reshape(STRIDE, STRIDE, image_count, height // STRIDE, breadth // STRIDE, channels)
    dilated = dilated.transpose(2, 3, 0, 4, 1, 5).reshape(latent.shape)
    mixing = blend_weight[None, :, :, None]
    mixed_rows = ((1.0 - mixing) * local_out + mixing * dilated.astype(jnp.float32)).astype(jnp.bfloat16)
    attention = jnp.dot(mixed_rows.reshape(-1, channels), w_out, preferred_element_type=jnp.float32).reshape(latent.shape)
    upsampled = jnp.repeat(jnp.repeat(previous, 2, axis=1), 2, axis=2).astype(jnp.float32)
    keeping = skip_weight[None, :, :, None]
    return ((1.0 - keeping) * (latent.astype(jnp.float32) + attention) + keeping * upsampled).astype(jnp.bfloat16)
```

```python
import functools

import jax
import jax.numpy as jnp
from jax import lax
from jax.experimental import pallas as pl
from jax.experimental.pallas import tpu as pltpu
from jax.sharding import PartitionSpec as P

HEADS = 10
HD = 64
C = 640
TOK = 512
CHUNK = 512
WIN = 3072
SUB = 4096
ROWS = 1024
AUG = 80
NEG = -1e30
SCALE = 0.125 * 1.4426950408889634
MESH = pl.DeviceIdType.MESH
BF = jnp.bfloat16
F32 = jnp.float32


def dot(a, b):
    return jnp.dot(a, b, preferred_element_type=F32)


def dot_nt(a, b):
    return lax.dot_general(a, b, (((1,), (1,)), ((), ())), preferred_element_type=F32)


def pipeline(count, scores, weigh):
    scores(0, 0)
    loops = (count - 1) // 2

    def body(i, carry):
        scores(2 * i + 1, 1)
        weigh(2 * i, 0)
        scores(2 * i + 2, 0)
        weigh(2 * i + 1, 1)
        return carry

    if loops:
        lax.fori_loop(0, loops, body, 0)
    if count % 2:
        weigh(count - 1, 0)
    else:
        scores(count - 1, 1)
        weigh(count - 2, 0)
        weigh(count - 1, 1)


def kernel(
    latent_ref, previous_ref, blend_ref, skip_ref, gain_ref, wq_ref, wk_ref, wv_ref, wo_ref,
    out_ref,
    wqt, wvt, nrm, halo_lr, halo_s, gat, qpad, kwin, vaug, acc, run_max, s_buf, s_max,
    wkd, wqd, wvd, qd, kd, vaug_d, acc_d, max_d, dil, ret, local,
    a2a_send, a2a_recv, halo_send, halo_recv, z_send, z_recv, c_send, c_recv, r_send, r_recv,
):
    t, p = lax.axis_index("tile"), lax.axis_index("phase")
    z, y_hi = t % 4, t // 4
    x, y_lo, core = p // 4, (p // 2) % 2, p % 2
    me = x * 4 + y_hi * 2 + y_lo

    def column(s, c):
        return ((s // 2) % 2 * 4 + z, s // 4 * 4 + s % 2 * 2 + c)

    up, down = ((t + 7) % 8, p), ((t + 1) % 8, p)
    left, right = (t, (p + 15) % 16), (t, (p + 1) % 16)
    z_next, z_prev = (y_hi * 4 + (z + 1) % 4, p), (y_hi * 4 + (z + 3) % 4, p)
    other = (t, p + 1 - 2 * core)

    barrier = pltpu.get_barrier_semaphore()
    for device in (up, down, left, right, z_next, z_prev):
        pl.semaphore_signal(barrier, inc=1, device_id=device, device_id_type=MESH)

    def greet(k, carry):
        pl.semaphore_signal(
            barrier, inc=1, device_id=column((me + k // 2) % 16, (core + k) % 2), device_id_type=MESH
        )
        return carry

    lax.fori_loop(1, 32, greet, 0)

    def order(shape, dim):
        r = lax.broadcasted_iota(jnp.int32, shape, dim)
        f, k = r // 32, r % 32
        return (4 * (k // 4) + f // 4) * 16 + 4 * (k % 4) + f % 4

    wide = latent_ref[...].astype(F32)
    average = jnp.mean(wide, axis=-1, keepdims=True)
    centred = wide - average
    variance = jnp.mean(centred * centred, axis=-1, keepdims=True)
    natural = (centred * lax.rsqrt(variance + 1e-5) * gain_ref[...]).astype(BF)
    pick = jnp.where(
        order((TOK, TOK), 0) == lax.broadcasted_iota(jnp.int32, (TOK, TOK), 1), 1.0, 0.0
    ).astype(BF)
    nrm[...] = dot(pick, natural).astype(BF).reshape(16, 32, C)

    pl.semaphore_wait(barrier, 37)

    def remote(src, dst, send, recv, device):
        return pltpu.make_async_remote_copy(
            src_ref=src, dst_ref=dst, send_sem=send, recv_sem=recv, device_id=device, device_id_type=MESH
        )

    def halo(i):
        if i < 2:
            return remote(nrm, halo_lr.at[i], halo_send.at[i], halo_recv.at[i], (right, left)[i])
        if i == 2:
            src, device = nrm.at[:, pl.ds(16, 16)], down
        elif i == 3:
            src, device = nrm.at[:, pl.ds(0, 16)], up
        else:
            src, device = halo_s.at[(i - 4) // 2], (right, left)[i % 2]
        return remote(src, halo_s.at[i - 2], halo_send.at[i], halo_recv.at[i], device)

    def exchange(k):
        to = (me + k) % 16
        return remote(
            nrm.at[to], gat.at[z, core, me], a2a_send.at[k], a2a_recv.at[k], column(to, core)
        )

    def exchanged(k):
        return remote(
            nrm.at[0], gat.at[z, core, (me + 16 - k) % 16], a2a_send.at[k], a2a_recv.at[k], column(me, core)
        )

    def ring(i):
        if i < 2:
            shard = gat.at[z, core]
        else:
            shard = gat.at[(z + (3, 1)[i - 2]) % 4, core, pl.ds(8 * (i - 2), 8)]
        return remote(shard, shard, z_send.at[i], z_recv.at[i], (z_next, z_prev)[i % 2])

    def ringed(i):
        if i < 2:
            shard = gat.at[(z + (3, 1)[i]) % 4, core]
        else:
            shard = gat.at[(z + 2) % 4, core, pl.ds(8 * (i - 2), 8)]
        return remote(shard, shard, z_send.at[i], z_recv.at[i], (z_next, z_prev)[i % 2])

    def across(i):
        shard = gat.at[(z + (0, 3, 1, 2)[i]) % 4, core]
        return remote(shard, shard, c_send.at[i], c_recv.at[i], other)

    def crossed(i):
        shard = gat.at[(z + (0, 3, 1, 2)[i]) % 4, 1 - core]
        return remote(shard, shard, c_send.at[i], c_recv.at[i], other)

    def each(first, last, act):
        def body(k, carry):
            act(k)
            return carry

        lax.fori_loop(first, last, body, 0)

    halo(2).start()
    halo(3).start()
    each(1, 16, lambda k: exchange(k).start())
    halo(0).start()
    halo(1).start()
    gat[z, core, me] = nrm[me]

    wqt[...] = wq_ref[...].T
    wvt[...] = wv_ref[...].T
    vaug[:, HD:, :] = jnp.ones((HEADS, AUG - HD, WIN), BF)
    vaug_d[:, HD:, :] = jnp.ones((5, AUG - HD, SUB), BF)

    own = nrm[...].reshape(TOK, C)
    queries = dot_nt(wqt[...], own).astype(BF)
    zeros = jnp.zeros((HD, TOK), BF)
    for j in range(5):
        first, second = queries[j * 128 : j * 128 + HD], queries[j * 128 + HD : j * 128 + 128]
        qpad[j, :HD, :TOK] = first
        qpad[j, HD:, :TOK] = zeros
        qpad[j, :HD, TOK:] = zeros
        qpad[j, HD:, TOK:] = second

    def window(tokens, chunk):
        at = pl.multiple_of(chunk * CHUNK, CHUNK)
        kwin[pl.ds(at, CHUNK), :] = dot(tokens, wk_ref[...]).astype(BF)
        vaug[:, :HD, pl.ds(at, CHUNK)] = dot_nt(wvt[...], tokens).astype(BF).reshape(HEADS, HD, CHUNK)

    top, bottom, west, east = t == 0, t == 7, p == 0, p == 15

    def penalties(chunk):
        outside_a = (
            (top & ((chunk == 3) | (chunk == 4)))
            | (bottom & (chunk == 5))
            | (west & ((chunk == 1) | (chunk == 4) | (chunk == 5)))
            | (east & (chunk == 2))
        )
        outside_b = (
            (bottom & ((chunk == 3) | (chunk == 5)))
            | (top & (chunk == 4))
            | (west & (chunk == 1))
            | (east & ((chunk == 2) | (chunk == 4) | (chunk == 5)))
        )
        return jnp.where(outside_a, -NEG, 0.0), jnp.where(outside_b, -NEG, 0.0)

    half = CHUNK // 2

    def attend_window(base, chunks):
        def place(i):
            return i // chunks, base + i % chunks

        def scores(i, slot):
            pair, chunk = place(i)
            s = dot(
                kwin[pl.ds(pl.multiple_of(chunk * CHUNK, CHUNK), CHUNK), pl.ds(pl.multiple_of(pair * 128, 128), 128)],
                qpad[pair],
            )
            s_buf[slot] = s
            pen_a, pen_b = penalties(chunk)
            s_max[slot, 0:1, :] = jnp.maximum(
                jnp.max(s[:half], axis=0, keepdims=True) - pen_a, jnp.max(s[half:], axis=0, keepdims=True) - pen_b
            )

        def weigh(i, slot):
            pair, chunk = place(i)
            pen_a, pen_b = penalties(chunk)
            if base == 0:
                new = s_max[slot, 0:1, :]
            else:
                old = run_max[pair, 0:1, :]
                new = jnp.maximum(old, s_max[slot, 0:1, :])
                fade = jnp.exp2((old - new) * SCALE)
            run_max[pair, 0:1, :] = new
            s = s_buf[slot]
            weights = jnp.concatenate(
                [
                    jnp.exp2(((s[:half] - (new + pen_a)) * SCALE).astype(BF)),
                    jnp.exp2(((s[half:] - (new + pen_b)) * SCALE).astype(BF)),
                ],
                axis=0,
            )
            at = pl.multiple_of(chunk * CHUNK, CHUNK)
            for b in range(2):
                h = 2 * pair + b
                cols = slice(b * TOK, (b + 1) * TOK)
                part = dot(vaug[h, :, pl.ds(at, CHUNK)], weights[:, cols])
                if base:
                    part = acc[h] * fade[:, cols] + part
                acc[h] = part

        pipeline(5 * chunks, scores, weigh)

    window(own, 0)
    attend_window(0, 1)

    each(1, 16, lambda k: exchanged(k).wait_recv())
    for i in range(2):
        ring(i).start()
    across(0).start()
    for i in (2, 3):
        halo(i).wait_recv()
    for i in range(4, 8):
        halo(i).start()
    for i in (0, 1):
        halo(i).wait_recv()
    each(1, 3, lambda c: window(halo_lr[c - 1].reshape(CHUNK, C), c))
    attend_window(1, 2)

    for i in (0, 1):
        ringed(i).wait_recv()
        ring(2 + i).start()
        across(1 + i).start()
    for i in range(4, 8):
        halo(i).wait_recv()
    each(3, 6, lambda c: window(halo_s[pl.ds(2 * (c - 3), 2)].reshape(CHUNK, C), c))
    attend_window(3, 3)

    for i in (2, 3):
        ringed(i).wait_recv()
    across(3).start()

    for j in range(5):
        both = [acc[2 * j + b, :HD] / acc[2 * j + b, HD : HD + 1] for b in range(2)]
        local[:, j * 128 : (j + 1) * 128] = jnp.concatenate(both, axis=0).T

    wkd[:, :256] = wk_ref[:, pl.ds(pl.multiple_of(core * 384, 128), 256)]
    wkd[:, 256:] = wk_ref[:, 256:384]
    wqd[:256] = wqt[pl.ds(pl.multiple_of(core * 384, 128), 256), :]
    wqd[256:] = wqt[pl.ds(pl.multiple_of(256 + core * 64, 64), HD), :]
    wvd[:256] = wvt[pl.ds(pl.multiple_of(core * 384, 128), 256), :]
    wvd[256:] = wvt[pl.ds(pl.multiple_of(256 + core * 64, 64), HD), :]
    qd[...] = jnp.zeros_like(qd)

    for c in range(2):
        if c == 0:
            for i in range(4):
                crossed(i).wait_recv()
        tokens = gat[z, c].reshape(CHUNK, C)
        part = dot_nt(wqd[...], tokens).astype(BF)
        cols = slice(c * CHUNK, (c + 1) * CHUNK)
        for i in range(4):
            qd[i, i % 2 * HD : i % 2 * HD + HD, cols] = part[i * HD : (i + 1) * HD]
        qd[4, pl.ds(pl.multiple_of(core * HD, HD), HD), cols] = part[256:]

    def sub_chunk(g):
        tokens = gat[g // 2, g % 2].reshape(CHUNK, C)
        at = pl.multiple_of(g * CHUNK, CHUNK)
        keys = dot(tokens, wkd[...]).astype(BF)
        for j in range(3):
            kd[j, pl.ds(at, CHUNK), :] = keys[:, j * 128 : (j + 1) * 128]
        vaug_d[:, :HD, pl.ds(at, CHUNK)] = dot_nt(wvd[...], tokens).astype(BF).reshape(5, HD, CHUNK)

    each(0, 8, sub_chunk)

    def give(j, k):
        s, c = (me + k // 2) % 16, (core + k) % 2
        return remote(
            dil.at[j, c * 16 + s], ret.at[core, j, me], r_send.at[j, k], r_recv.at[j, k], column(s, c)
        )

    def given(j, k):
        s, c = (me + 16 - k // 2) % 16, (core + k) % 2
        return remote(dil.at[j, 0], ret.at[c, j, s], r_send.at[j, k], r_recv.at[j, k], column(me, core))

    def attend_sub(first, heads):
        def scores(i, slot):
            h, g = first + i // 8, i % 8
            s = dot(kd[h // 2, pl.ds(pl.multiple_of(g * CHUNK, CHUNK), CHUNK), :], qd[h])
            s_buf[slot] = s
            s_max[slot, 0:1, :] = jnp.max(s, axis=0, keepdims=True)

        def weigh(i, slot):
            h, g = first + i // 8, i % 8
            old = max_d[h, 0:1, :]
            new = jnp.maximum(old, s_max[slot, 0:1, :])
            fade = jnp.exp2((old - new) * SCALE)
            max_d[h, 0:1, :] = new
            weights = jnp.exp2(((s_buf[slot] - new) * SCALE).astype(BF))
            values = vaug_d[h, :, pl.ds(pl.multiple_of(g * CHUNK, CHUNK), CHUNK)]
            for b in range(2):
                cols = slice(b * TOK, (b + 1) * TOK)
                acc_d[h, :, cols] = acc_d[h, :, cols] * fade[:, cols] + dot(values, weights[:, cols])

        pipeline(8 * heads, scores, weigh)

    max_d[...] = jnp.full_like(max_d, NEG)
    acc_d[...] = jnp.zeros_like(acc_d)
    for j in range(3):
        attend_sub(2 * j, 2 if j < 2 else 1)
        if j < 2:
            both = [acc_d[2 * j + b, :HD] / acc_d[2 * j + b, HD : HD + 1] for b in range(2)]
        else:
            only = acc_d[4, :HD] / acc_d[4, HD : HD + 1]
            both = [jnp.where(core == b, only, 0.0) for b in range(2)]
        dil[j] = jnp.concatenate(both, axis=0).T.astype(BF).reshape(32, 32, 128)
        each(1, 32, lambda k: give(j, k).start())
        ret[core, j, me] = dil[j, core * 16 + me]

    def position(ref, natural_of):
        rows = jnp.where(
            natural_of((TOK, 32), 0) // 16 == lax.broadcasted_iota(jnp.int32, (TOK, 32), 1), 1.0, 0.0
        )
        spread = jnp.dot(rows, ref[...], preferred_element_type=F32, precision=lax.Precision.HIGHEST)
        here = natural_of((TOK, 16), 0) % 16 == lax.broadcasted_iota(jnp.int32, (TOK, 16), 1)
        return jnp.sum(jnp.where(here, spread, 0.0), axis=1, keepdims=True)

    def plain(shape, dim):
        return lax.broadcasted_iota(jnp.int32, shape, dim)

    mixing = position(blend_ref, order)
    keeping = position(skip_ref, plain)
    token = plain((TOK, 128), 0)
    source = token // 32 * 8 + token % 16 // 2
    repeat = jnp.where(source == lax.broadcasted_iota(jnp.int32, (TOK, 128), 1), 1.0, 0.0).astype(BF)
    upsampled = dot(repeat, previous_ref[...])
    place_back = jnp.where(
        order((TOK, TOK), 1) == lax.broadcasted_iota(jnp.int32, (TOK, TOK), 0), 1.0, 0.0
    ).astype(BF)

    for j in range(3):
        each(1, 32, lambda k: given(j, k).wait_recv())

    columns = []
    for pair in range(5):
        if pair == 2:
            dilated = ret[0, 2].astype(F32) + ret[1, 2].astype(F32)
        else:
            dilated = ret[pair // 3, pair % 3].astype(F32)
        dilated = dilated.reshape(TOK, 128)
        columns.append(
            ((1.0 - mixing) * local[:, pair * 128 : (pair + 1) * 128] + mixing * dilated).astype(BF)
        )
    mixed = dot(place_back, jnp.concatenate(columns, axis=1)).astype(BF)
    attention = dot(mixed, wo_ref[...])
    out_ref[...] = (
        (1.0 - keeping) * (latent_ref[...].astype(F32) + attention) + keeping * upsampled
    ).astype(BF)

    each(1, 16, lambda k: exchange(k).wait_send())
    for i in range(8):
        halo(i).wait_send()
    for i in range(4):
        ring(i).wait_send()
        across(i).wait_send()
    for j in range(3):
        each(1, 32, lambda k: give(j, k).wait_send())


def shards(latent, previous, blend_weight, skip_weight, norm_gain, w_query, w_key, w_value, w_out):
    vmem = pltpu.VMEM
    dma = pltpu.SemaphoreType.DMA
    result = pl.pallas_call(
        kernel,
        out_shape=jax.ShapeDtypeStruct((TOK, C), BF),
        in_specs=[pl.BlockSpec(memory_space=pltpu.VMEM)] * 9,
        out_specs=pl.BlockSpec(memory_space=pltpu.VMEM),
        scratch_shapes=[
            vmem((C, C), BF),
            vmem((C, C), BF),
            vmem((16, 32, C), BF),
            vmem((2, 16, 32, C), BF),
            vmem((6, 16, 16, C), BF),
            vmem((4, 2, 16, 32, C), BF),
            vmem((5, 128, ROWS), BF),
            vmem((WIN, C), BF),
            vmem((HEADS, AUG, WIN), BF),
            vmem((HEADS, AUG, TOK), F32),
            vmem((5, 8, ROWS), F32),
            vmem((2, CHUNK, ROWS), F32),
            vmem((2, 8, ROWS), F32),
            vmem((C, 384), BF),
            vmem((320, C), BF),
            vmem((320, C), BF),
            vmem((5, 128, ROWS), BF),
            vmem((3, SUB, 128), BF),
            vmem((5, AUG, SUB), BF),
            vmem((5, AUG, ROWS), F32),
            vmem((5, 8, ROWS), F32),
            vmem((3, 32, 32, 128), BF),
            vmem((2, 3, 16, 32, 128), BF),
            vmem((TOK, C), F32),
            dma((16,)), dma((16,)), dma((8,)), dma((8,)), dma((4,)), dma((4,)), dma((4,)), dma((4,)),
            dma((3, 32)), dma((3, 32)),
        ],
        compiler_params=pltpu.CompilerParams(
            collective_id=0, has_side_effects=True, vmem_limit_bytes=60 * 2**20
        ),
    )(
        latent.reshape(TOK, C), previous.reshape(128, C), blend_weight, skip_weight,
        norm_gain.reshape(1, C), w_query, w_key, w_value, w_out,
    )
    return result.reshape(latent.shape)


def solution(mesh):
    return jax.shard_map(
        shards,
        mesh=mesh,
        in_specs=(
            P(None, "tile", "phase", None),
            P(None, "tile", "phase", None),
            P("tile", "phase"),
            P("tile", "phase"),
            P(),
            P(),
            P(),
            P(),
            P(),
        ),
        out_specs=P(None, "tile", "phase", None),
        check_vma=False,
    )
```

```python
import functools

import jax
import jax.numpy as jnp
from jax import lax
from jax.experimental import pallas as pl
from jax.experimental.pallas import tpu as pltpu
from jax.sharding import PartitionSpec as P

HEADS = 10
HD = 64
C = 640
TOK = 512
CHUNK = 512
WIN = 3072
SUB = 4096
ROWS = 1024
AUG = 80
NEG = -1e30
SCALE = 0.125 * 1.4426950408889634
MESH = pl.DeviceIdType.MESH
BF = jnp.bfloat16
F32 = jnp.float32


def dot(a, b):
    return jnp.dot(a, b, preferred_element_type=F32)


def dot_nt(a, b):
    return lax.dot_general(a, b, (((1,), (1,)), ((), ())), preferred_element_type=F32)


def pipeline(count, scores, weigh):
    scores(0, 0)
    loops = (count - 1) // 2

    def body(i, carry):
        scores(2 * i + 1, 1)
        weigh(2 * i, 0)
        scores(2 * i + 2, 0)
        weigh(2 * i + 1, 1)
        return carry

    if loops:
        lax.fori_loop(0, loops, body, 0)
    if count % 2:
        weigh(count - 1, 0)
    else:
        scores(count - 1, 1)
        weigh(count - 2, 0)
        weigh(count - 1, 1)


def kernel(
    latent_ref, previous_ref, blend_ref, skip_ref, gain_ref, wq_ref, wk_ref, wv_ref, wo_ref,
    out_ref,
    wqt, wvt, nrm, halo_lr, halo_s, gat, qpad, kwin, vaug, acc, run_max, s_buf, s_max,
    wkd, wqd, wvd, qd, kd, vaug_d, acc_d, max_d, dil, ret, local,
    a2a_send, a2a_recv, halo_send, halo_recv, z_send, z_recv, c_send, c_recv, r_send, r_recv,
):
    t, p = lax.axis_index("tile"), lax.axis_index("phase")
    z, y_hi = t % 4, t // 4
    x, y_lo, core = p // 4, (p // 2) % 2, p % 2
    me = x * 4 + y_hi * 2 + y_lo

    def column(s, c):
        return ((s // 2) % 2 * 4 + z, s // 4 * 4 + s % 2 * 2 + c)

    up, down = ((t + 7) % 8, p), ((t + 1) % 8, p)
    far = (t, (p + 15 + 2 * core) % 16)
    z_next, z_prev = (y_hi * 4 + (z + 1) % 4, p), (y_hi * 4 + (z + 3) % 4, p)
    other = (t, p + 1 - 2 * core)

    barrier = pltpu.get_barrier_semaphore()
    for device in (up, down, far, z_next, z_prev):
        pl.semaphore_signal(barrier, inc=1, device_id=device, device_id_type=MESH)

    def greet(k, carry):
        pl.semaphore_signal(
            barrier, inc=1, device_id=column((me + k // 2) % 16, (core + k) % 2), device_id_type=MESH
        )
        return carry

    lax.fori_loop(1, 32, greet, 0)

    def order(shape, dim):
        r = lax.broadcasted_iota(jnp.int32, shape, dim)
        f, k = r // 32, r % 32
        return (4 * (k // 4) + f // 4) * 16 + 4 * (k % 4) + f % 4

    wide = latent_ref[...].astype(F32)
    average = jnp.mean(wide, axis=-1, keepdims=True)
    centred = wide - average
    variance = jnp.mean(centred * centred, axis=-1, keepdims=True)
    natural = (centred * lax.rsqrt(variance + 1e-5) * gain_ref[...][None, :]).astype(BF)
    pick = jnp.where(
        order((TOK, TOK), 0) == lax.broadcasted_iota(jnp.int32, (TOK, TOK), 1), 1.0, 0.0
    ).astype(BF)
    nrm[...] = dot(pick, natural).astype(BF).reshape(16, 32, C)

    pl.semaphore_wait(barrier, 36)

    def remote(src, dst, send, recv, device):
        return pltpu.make_async_remote_copy(
            src_ref=src, dst_ref=dst, send_sem=send, recv_sem=recv, device_id=device, device_id_type=MESH
        )

    def halo(i):
        if i < 2:
            return remote(nrm, halo_lr.at[i], halo_send.at[i], halo_recv.at[i], (other, far)[i])
        if i == 2:
            src, device = nrm.at[:, pl.ds(16, 16)], down
        elif i == 3:
            src, device = nrm.at[:, pl.ds(0, 16)], up
        else:
            src, device = halo_s.at[i % 2], (other, far)[(i - 4) // 2]
        return remote(src, halo_s.at[i - 2], halo_send.at[i], halo_recv.at[i], device)

    def exchange(k):
        to = (me + k) % 16
        return remote(
            nrm.at[to], gat.at[z, core, me], a2a_send.at[k], a2a_recv.at[k], column(to, core)
        )

    def exchanged(k):
        return remote(
            nrm.at[0], gat.at[z, core, (me + 16 - k) % 16], a2a_send.at[k], a2a_recv.at[k], column(me, core)
        )

    def ring(i):
        if i < 2:
            shard = gat.at[z, core]
        else:
            shard = gat.at[(z + (3, 1)[i - 2]) % 4, core, pl.ds(8 * (i - 2), 8)]
        return remote(shard, shard, z_send.at[i], z_recv.at[i], (z_next, z_prev)[i % 2])

    def ringed(i):
        if i < 2:
            shard = gat.at[(z + (3, 1)[i]) % 4, core]
        else:
            shard = gat.at[(z + 2) % 4, core, pl.ds(8 * (i - 2), 8)]
        return remote(shard, shard, z_send.at[i], z_recv.at[i], (z_next, z_prev)[i % 2])

    def across(i):
        shard = gat.at[(z + (0, 3, 1, 2)[i]) % 4, core]
        return remote(shard, shard, c_send.at[i], c_recv.at[i], other)

    def crossed(i):
        shard = gat.at[(z + (0, 3, 1, 2)[i]) % 4, 1 - core]
        return remote(shard, shard, c_send.at[i], c_recv.at[i], other)

    def each(first, last, act):
        def body(k, carry):
            act(k)
            return carry

        lax.fori_loop(first, last, body, 0)

    halo(2).start()
    halo(3).start()
    each(1, 16, lambda k: exchange(k).start())
    halo(0).start()
    gat[z, core, me] = nrm[me]

    wqt[...] = wq_ref[...].T
    wvt[...] = wv_ref[...].T
    vaug[:, HD:, :] = jnp.ones((HEADS, AUG - HD, WIN), BF)
    vaug_d[:, HD:, :] = jnp.ones((5, AUG - HD, SUB), BF)

    own = nrm[...].reshape(TOK, C)
    queries = dot_nt(wqt[...], own).astype(BF)
    zeros = jnp.zeros((HD, TOK), BF)
    for j in range(5):
        first, second = queries[j * 128 : j * 128 + HD], queries[j * 128 + HD : j * 128 + 128]
        qpad[j, :HD, :TOK] = first
        qpad[j, HD:, :TOK] = zeros
        qpad[j, :HD, TOK:] = zeros
        qpad[j, HD:, TOK:] = second

    def window(tokens, chunk):
        at = pl.multiple_of(chunk * CHUNK, CHUNK)
        kwin[pl.ds(at, CHUNK), :] = dot(tokens, wk_ref[...]).astype(BF)
        vaug[:, :HD, pl.ds(at, CHUNK)] = dot_nt(wvt[...], tokens).astype(BF).reshape(HEADS, HD, CHUNK)

    top, bottom = t == 0, t == 7
    edge = ((core == 0) & (p == 0)) | ((core == 1) & (p == 15))

    def penalties(chunk):
        corner = (chunk == 2) | (chunk == 3) | (chunk == 5)
        beyond = edge & (chunk >= 4)
        return (
            jnp.where((top & corner) | beyond, -NEG, 0.0),
            jnp.where((bottom & corner) | beyond, -NEG, 0.0),
        )

    half = CHUNK // 2

    def attend_window(base, chunks):
        def place(i):
            return i // chunks, base + i % chunks

        def scores(i, slot):
            pair, chunk = place(i)
            s = dot(
                kwin[pl.ds(pl.multiple_of(chunk * CHUNK, CHUNK), CHUNK), pl.ds(pl.multiple_of(pair * 128, 128), 128)],
                qpad[pair],
            )
            s_buf[slot] = s
            pen_a, pen_b = penalties(chunk)
            s_max[slot, 0:1, :] = jnp.maximum(
                jnp.max(s[:half], axis=0, keepdims=True) - pen_a, jnp.max(s[half:], axis=0, keepdims=True) - pen_b
            )

        def weigh(i, slot):
            pair, chunk = place(i)
            pen_a, pen_b = penalties(chunk)
            if base == 0:
                new = s_max[slot, 0:1, :]
            else:
                old = run_max[pair, 0:1, :]
                new = jnp.maximum(old, s_max[slot, 0:1, :])
                fade = jnp.exp2((old - new) * SCALE)
            run_max[pair, 0:1, :] = new
            s = s_buf[slot]
            weights = jnp.concatenate(
                [
                    jnp.exp2(((s[:half] - (new + pen_a)) * SCALE).astype(BF)),
                    jnp.exp2(((s[half:] - (new + pen_b)) * SCALE).astype(BF)),
                ],
                axis=0,
            )
            at = pl.multiple_of(chunk * CHUNK, CHUNK)
            for b in range(2):
                h = 2 * pair + b
                cols = slice(b * TOK, (b + 1) * TOK)
                part = dot(vaug[h, :, pl.ds(at, CHUNK)], weights[:, cols])
                if base:
                    part = acc[h] * fade[:, cols] + part
                acc[h] = part

        pipeline(5 * chunks, scores, weigh)

    window(own, 0)
    attend_window(0, 1)
    halo(0).wait_recv()
    window(halo_lr[0].reshape(CHUNK, C), 1)
    attend_window(1, 1)

    each(1, 16, lambda k: exchanged(k).wait_recv())
    for i in range(2):
        ring(i).start()
    across(0).start()
    halo(1).start()
    for i in (2, 3):
        halo(i).wait_recv()
    for i in range(4, 8):
        halo(i).start()
    window(halo_s[:2].reshape(CHUNK, C), 2)
    for i in (4, 5):
        halo(i).wait_recv()
    window(halo_s[2:4].reshape(CHUNK, C), 3)
    attend_window(2, 2)

    wkd[:, :256] = wk_ref[:, pl.ds(pl.multiple_of(core * 384, 128), 256)]
    wkd[:, 256:] = wk_ref[:, 256:384]
    wqd[:256] = wqt[pl.ds(pl.multiple_of(core * 384, 128), 256), :]
    wqd[256:] = wqt[pl.ds(pl.multiple_of(256 + core * 64, 64), HD), :]
    wvd[:256] = wvt[pl.ds(pl.multiple_of(core * 384, 128), 256), :]
    wvd[256:] = wvt[pl.ds(pl.multiple_of(256 + core * 64, 64), HD), :]
    qd[...] = jnp.zeros_like(qd)
    max_d[...] = jnp.full_like(max_d, NEG)
    acc_d[...] = jnp.zeros_like(acc_d)

    crossed(0).wait_recv()
    for c in range(2):
        tokens = gat[z, c].reshape(CHUNK, C)
        part = dot_nt(wqd[...], tokens).astype(BF)
        cols = slice(c * CHUNK, (c + 1) * CHUNK)
        for i in range(4):
            qd[i, i % 2 * HD : i % 2 * HD + HD, cols] = part[i * HD : (i + 1) * HD]
        qd[4, pl.ds(pl.multiple_of(core * HD, HD), HD), cols] = part[256:]

    def sub_chunk(g):
        plane = jnp.where(g < 2, 0, jnp.where(g > 5, 2, jnp.where(g % 2 == 0, 3, 1)))
        own_core = (g == 0) | (g == 2) | (g == 3) | (g == 6)
        tokens = gat[(z + plane) % 4, jnp.where(own_core, core, 1 - core)].reshape(CHUNK, C)
        at = pl.multiple_of(g * CHUNK, CHUNK)
        keys = dot(tokens, wkd[...]).astype(BF)
        for j in range(3):
            kd[j, pl.ds(at, CHUNK), :] = keys[:, j * 128 : (j + 1) * 128]
        vaug_d[:, :HD, pl.ds(at, CHUNK)] = dot_nt(wvd[...], tokens).astype(BF).reshape(5, HD, CHUNK)

    def give(j, k):
        s, c = (me + k // 2) % 16, (core + k) % 2
        return remote(
            dil.at[j, c * 16 + s], ret.at[core, j, me], r_send.at[j, k], r_recv.at[j, k], column(s, c)
        )

    def given(j, k):
        s, c = (me + 16 - k // 2) % 16, (core + k) % 2
        return remote(dil.at[j, 0], ret.at[c, j, s], r_send.at[j, k], r_recv.at[j, k], column(me, core))

    def attend_sub(first, heads, base, chunks):
        def place(i):
            return first + i // chunks, base + i % chunks

        def scores(i, slot):
            h, g = place(i)
            s = dot(kd[h // 2, pl.ds(pl.multiple_of(g * CHUNK, CHUNK), CHUNK), :], qd[h])
            s_buf[slot] = s
            s_max[slot, 0:1, :] = jnp.max(s, axis=0, keepdims=True)

        def weigh(i, slot):
            h, g = place(i)
            old = max_d[h, 0:1, :]
            new = jnp.maximum(old, s_max[slot, 0:1, :])
            fade = jnp.exp2((old - new) * SCALE)
            max_d[h, 0:1, :] = new
            weights = jnp.exp2(((s_buf[slot] - new) * SCALE).astype(BF))
            values = vaug_d[h, :, pl.ds(pl.multiple_of(g * CHUNK, CHUNK), CHUNK)]
            for b in range(2):
                cols = slice(b * TOK, (b + 1) * TOK)
                acc_d[h, :, cols] = acc_d[h, :, cols] * fade[:, cols] + dot(values, weights[:, cols])

        pipeline(chunks * heads, scores, weigh)

    each(0, 2, sub_chunk)
    attend_sub(0, 5, 0, 2)

    for i in (0, 1):
        ringed(i).wait_recv()
        ring(2 + i).start()
        across(1 + i).start()
    each(2, 4, sub_chunk)
    attend_sub(0, 5, 2, 2)

    halo(1).wait_recv()
    window(halo_lr[1].reshape(CHUNK, C), 4)
    attend_window(4, 1)
    for i in (2, 3):
        ringed(i).wait_recv()
    across(3).start()
    for i in (6, 7):
        halo(i).wait_recv()
    window(halo_s[4:].reshape(CHUNK, C), 5)
    attend_window(5, 1)
    for j in range(5):
        both = [acc[2 * j + b, :HD] / acc[2 * j + b, HD : HD + 1] for b in range(2)]
        local[:, j * 128 : (j + 1) * 128] = jnp.concatenate(both, axis=0).T

    for i in (1, 2):
        crossed(i).wait_recv()
    each(4, 7, sub_chunk)
    crossed(3).wait_recv()
    sub_chunk(7)
    for j in range(3):
        attend_sub(2 * j, 2 if j < 2 else 1, 4, 4)
        if j < 2:
            both = [acc_d[2 * j + b, :HD] / acc_d[2 * j + b, HD : HD + 1] for b in range(2)]
        else:
            only = acc_d[4, :HD] / acc_d[4, HD : HD + 1]
            both = [jnp.where(core == b, only, 0.0) for b in range(2)]
        dil[j] = jnp.concatenate(both, axis=0).T.astype(BF).reshape(32, 32, 128)
        each(1, 32, lambda k: give(j, k).start())
        ret[core, j, me] = dil[j, core * 16 + me]

    def position(ref, natural_of):
        cols = jnp.where(
            natural_of((TOK, 16), 0) % 16 == lax.broadcasted_iota(jnp.int32, (TOK, 16), 1), 1.0, 0.0
        )
        spread = jnp.dot(cols, ref[...], preferred_element_type=F32, precision=lax.Precision.HIGHEST)
        here = natural_of((TOK, 32), 0) // 16 == lax.broadcasted_iota(jnp.int32, (TOK, 32), 1)
        return jnp.sum(jnp.where(here, spread, 0.0), axis=1, keepdims=True)

    def plain(shape, dim):
        return lax.broadcasted_iota(jnp.int32, shape, dim)

    mixing = position(blend_ref, order)
    keeping = position(skip_ref, plain)
    token = plain((TOK, 128), 0)
    source = token // 32 * 8 + token % 16 // 2
    repeat = jnp.where(source == lax.broadcasted_iota(jnp.int32, (TOK, 128), 1), 1.0, 0.0).astype(BF)
    upsampled = dot(repeat, previous_ref[...])
    place_back = jnp.where(
        order((TOK, TOK), 1) == lax.broadcasted_iota(jnp.int32, (TOK, TOK), 0), 1.0, 0.0
    ).astype(BF)

    for j in range(3):
        each(1, 32, lambda k: given(j, k).wait_recv())

    columns = []
    for pair in range(5):
        if pair == 2:
            dilated = ret[0, 2].astype(F32) + ret[1, 2].astype(F32)
        else:
            dilated = ret[pair // 3, pair % 3].astype(F32)
        dilated = dilated.reshape(TOK, 128)
        columns.append(
            ((1.0 - mixing) * local[:, pair * 128 : (pair + 1) * 128] + mixing * dilated).astype(BF)
        )
    mixed = dot(place_back, jnp.concatenate(columns, axis=1)).astype(BF)
    attention = dot(mixed, wo_ref[...])
    out_ref[...] = (
        (1.0 - keeping) * (latent_ref[...].astype(F32) + attention) + keeping * upsampled
    ).astype(BF)

    each(1, 16, lambda k: exchange(k).wait_send())
    for i in range(8):
        halo(i).wait_send()
    for i in range(4):
        ring(i).wait_send()
        across(i).wait_send()
    for j in range(3):
        each(1, 32, lambda k: give(j, k).wait_send())


def shards(latent, previous, blend_weight, skip_weight, norm_gain, w_query, w_key, w_value, w_out):
    vmem = pltpu.VMEM
    dma = pltpu.SemaphoreType.DMA
    result = pl.pallas_call(
        kernel,
        out_shape=jax.ShapeDtypeStruct((TOK, C), BF),
        in_specs=[pl.BlockSpec(memory_space=pltpu.VMEM)] * 9,
        out_specs=pl.BlockSpec(memory_space=pltpu.VMEM),
        scratch_shapes=[
            vmem((C, C), BF),
            vmem((C, C), BF),
            vmem((16, 32, C), BF),
            vmem((2, 16, 32, C), BF),
            vmem((6, 16, 16, C), BF),
            vmem((4, 2, 16, 32, C), BF),
            vmem((5, 128, ROWS), BF),
            vmem((WIN, C), BF),
            vmem((HEADS, AUG, WIN), BF),
            vmem((HEADS, AUG, TOK), F32),
            vmem((5, 8, ROWS), F32),
            vmem((2, CHUNK, ROWS), F32),
            vmem((2, 8, ROWS), F32),
            vmem((C, 384), BF),
            vmem((320, C), BF),
            vmem((320, C), BF),
            vmem((5, 128, ROWS), BF),
            vmem((3, SUB, 128), BF),
            vmem((5, AUG, SUB), BF),
            vmem((5, AUG, ROWS), F32),
            vmem((5, 8, ROWS), F32),
            vmem((3, 32, 32, 128), BF),
            vmem((2, 3, 16, 32, 128), BF),
            vmem((TOK, C), F32),
            dma((16,)), dma((16,)), dma((8,)), dma((8,)), dma((4,)), dma((4,)), dma((4,)), dma((4,)),
            dma((3, 32)), dma((3, 32)),
        ],
        compiler_params=pltpu.CompilerParams(
            collective_id=0, has_side_effects=True, vmem_limit_bytes=60 * 2**20
        ),
    )(
        latent.reshape(TOK, C), previous.reshape(128, C), blend_weight.T, skip_weight.T,
        norm_gain, w_query, w_key, w_value, w_out,
    )
    return result.reshape(latent.shape)


def solution(mesh):
    return jax.shard_map(
        shards,
        mesh=mesh,
        in_specs=(
            P(None, "tile", "phase", None),
            P(None, "tile", "phase", None),
            P("tile", "phase"),
            P("tile", "phase"),
            P(),
            P(),
            P(),
            P(),
            P(),
        ),
        out_specs=P(None, "tile", "phase", None),
        check_vma=False,
    )
```

```python
import functools

import jax
import jax.numpy as jnp
from jax import lax
from jax.experimental import pallas as pl
from jax.experimental.pallas import tpu as pltpu
from jax.sharding import PartitionSpec as P

HEADS = 10
HD = 64
C = 640
TOK = 512
CHUNK = 512
WIN = 3072
SUB = 4096
ROWS = 1024
AUG = 80
NEG = -1e30
SCALE = 0.125 * 1.4426950408889634
MESH = pl.DeviceIdType.MESH
BF = jnp.bfloat16
F32 = jnp.float32


def dot(a, b):
    return jnp.dot(a, b, preferred_element_type=F32)


def dot_nt(a, b):
    return lax.dot_general(a, b, (((1,), (1,)), ((), ())), preferred_element_type=F32)


def pipeline(count, scores, weigh):
    scores(0, 0)
    loops = (count - 1) // 2

    def body(i, carry):
        scores(2 * i + 1, 1)
        weigh(2 * i, 0)
        scores(2 * i + 2, 0)
        weigh(2 * i + 1, 1)
        return carry

    if loops:
        lax.fori_loop(0, loops, body, 0)
    if count % 2:
        weigh(count - 1, 0)
    else:
        scores(count - 1, 1)
        weigh(count - 2, 0)
        weigh(count - 1, 1)


def kernel(
    latent_ref, previous_ref, blend_ref, skip_ref, gain_ref, wq_ref, wk_ref, wv_ref, wo_ref,
    out_ref,
    wqt, wvt, nrm, halo_lr, halo_s, gat, qpad, kwin, vaug, acc, run_max, s_buf, s_max,
    wkd, wqd, wvd, qd, kd, vaug_d, acc_d, max_d, dil, ret, local,
    a2a_send, a2a_recv, halo_send, halo_recv, z_send, z_recv, c_send, c_recv, r_send, r_recv,
):
    t, p = lax.axis_index("tile"), lax.axis_index("phase")
    z, y_hi = t % 4, t // 4
    x, y_lo, core = p // 4, (p // 2) % 2, p % 2
    me = x * 4 + y_hi * 2 + y_lo

    def column(s, c):
        return ((s // 2) % 2 * 4 + z, s // 4 * 4 + s % 2 * 2 + c)

    up, down = ((t + 7) % 8, p), ((t + 1) % 8, p)
    far = (t, (p + 15 + 2 * core) % 16)
    z_next, z_prev = (y_hi * 4 + (z + 1) % 4, p), (y_hi * 4 + (z + 3) % 4, p)
    other = (t, p + 1 - 2 * core)

    barrier = pltpu.get_barrier_semaphore()
    for device in (up, down, far, z_next, z_prev):
        pl.semaphore_signal(barrier, inc=1, device_id=device, device_id_type=MESH)

    def greet(k, carry):
        pl.semaphore_signal(
            barrier, inc=1, device_id=column((me + k // 2) % 16, (core + k) % 2), device_id_type=MESH
        )
        return carry

    lax.fori_loop(1, 32, greet, 0)

    def order(shape, dim):
        r = lax.broadcasted_iota(jnp.int32, shape, dim)
        f, k = r // 32, r % 32
        return (4 * (k // 4) + f // 4) * 16 + 4 * (k % 4) + f % 4

    wide = latent_ref[...].astype(F32)
    average = jnp.mean(wide, axis=-1, keepdims=True)
    centred = wide - average
    variance = jnp.mean(centred * centred, axis=-1, keepdims=True)
    natural = (centred * lax.rsqrt(variance + 1e-5) * gain_ref[...][None, :]).astype(BF)
    pick = jnp.where(
        order((TOK, TOK), 0) == lax.broadcasted_iota(jnp.int32, (TOK, TOK), 1), 1.0, 0.0
    ).astype(BF)
    nrm[...] = dot(pick, natural).astype(BF).reshape(16, 32, C)

    pl.semaphore_wait(barrier, 36)

    def remote(src, dst, send, recv, device):
        return pltpu.make_async_remote_copy(
            src_ref=src, dst_ref=dst, send_sem=send, recv_sem=recv, device_id=device, device_id_type=MESH
        )

    def halo(i):
        if i < 2:
            return remote(nrm, halo_lr.at[i], halo_send.at[i], halo_recv.at[i], (other, far)[i])
        if i == 2:
            src, device = nrm.at[:, pl.ds(16, 16)], down
        elif i == 3:
            src, device = nrm.at[:, pl.ds(0, 16)], up
        else:
            src, device = halo_s.at[i % 2], (other, far)[(i - 4) // 2]
        return remote(src, halo_s.at[i - 2], halo_send.at[i], halo_recv.at[i], device)

    edge = ((core == 0) & (p == 0)) | ((core == 1) & (p == 15))
    above, below, beside = t > 0, t < 7, jnp.logical_not(edge)
    sends = (None, beside, below, above, above, below, above & beside, below & beside)
    receives = (None, beside, above, below, above, below, above & beside, below & beside)

    def when(condition, act):
        if condition is None:
            act()
        else:
            pl.when(condition)(act)

    def halo_start(i):
        when(sends[i], lambda: halo(i).start())

    def halo_sent(i):
        when(sends[i], lambda: halo(i).wait_send())

    def halo_here(i):
        when(receives[i], lambda: halo(i).wait_recv())
        if receives[i] is not None:

            @pl.when(jnp.logical_not(receives[i]))
            def _():
                if i < 2:
                    halo_lr[i] = jnp.zeros((16, 32, C), BF)
                else:
                    halo_s[i - 2] = jnp.zeros((16, 16, C), BF)

    def exchange(k):
        to = (me + k) % 16
        return remote(
            nrm.at[to], gat.at[z, core, me], a2a_send.at[k], a2a_recv.at[k], column(to, core)
        )

    def exchanged(k):
        return remote(
            nrm.at[0], gat.at[z, core, (me + 16 - k) % 16], a2a_send.at[k], a2a_recv.at[k], column(me, core)
        )

    def ring(i):
        if i < 2:
            shard = gat.at[z, core]
        else:
            shard = gat.at[(z + (3, 1)[i - 2]) % 4, core, pl.ds(8 * (i - 2), 8)]
        return remote(shard, shard, z_send.at[i], z_recv.at[i], (z_next, z_prev)[i % 2])

    def ringed(i):
        if i < 2:
            shard = gat.at[(z + (3, 1)[i]) % 4, core]
        else:
            shard = gat.at[(z + 2) % 4, core, pl.ds(8 * (i - 2), 8)]
        return remote(shard, shard, z_send.at[i], z_recv.at[i], (z_next, z_prev)[i % 2])

    def across(i):
        shard = gat.at[(z + (0, 3, 1, 2)[i]) % 4, core]
        return remote(shard, shard, c_send.at[i], c_recv.at[i], other)

    def crossed(i):
        shard = gat.at[(z + (0, 3, 1, 2)[i]) % 4, 1 - core]
        return remote(shard, shard, c_send.at[i], c_recv.at[i], other)

    def each(first, last, act):
        def body(k, carry):
            act(k)
            return carry

        lax.fori_loop(first, last, body, 0)

    halo_start(2)
    halo_start(3)
    each(1, 16, lambda k: exchange(k).start())
    halo_start(0)
    gat[z, core, me] = nrm[me]

    wqt[...] = wq_ref[...].T
    wvt[...] = wv_ref[...].T
    vaug[:, HD:, :] = jnp.ones((HEADS, AUG - HD, WIN), BF)
    vaug_d[:, HD:, :] = jnp.ones((5, AUG - HD, SUB), BF)

    own = nrm[...].reshape(TOK, C)
    queries = dot_nt(wqt[...], own).astype(BF)
    zeros = jnp.zeros((HD, TOK), BF)
    for j in range(5):
        first, second = queries[j * 128 : j * 128 + HD], queries[j * 128 + HD : j * 128 + 128]
        qpad[j, :HD, :TOK] = first
        qpad[j, HD:, :TOK] = zeros
        qpad[j, :HD, TOK:] = zeros
        qpad[j, HD:, TOK:] = second

    def window(tokens, chunk):
        at = pl.multiple_of(chunk * CHUNK, CHUNK)
        kwin[pl.ds(at, CHUNK), :] = dot(tokens, wk_ref[...]).astype(BF)
        vaug[:, :HD, pl.ds(at, CHUNK)] = dot_nt(wvt[...], tokens).astype(BF).reshape(HEADS, HD, CHUNK)

    top, bottom = t == 0, t == 7

    def penalties(chunk):
        corner = (chunk == 2) | (chunk == 3) | (chunk == 5)
        beyond = edge & (chunk >= 4)
        return (
            jnp.where((top & corner) | beyond, -NEG, 0.0),
            jnp.where((bottom & corner) | beyond, -NEG, 0.0),
        )

    half = CHUNK // 2

    def attend_window(base, chunks):
        def place(i):
            return i // chunks, base + i % chunks

        def scores(i, slot):
            pair, chunk = place(i)
            s = dot(
                kwin[pl.ds(pl.multiple_of(chunk * CHUNK, CHUNK), CHUNK), pl.ds(pl.multiple_of(pair * 128, 128), 128)],
                qpad[pair],
            )
            s_buf[slot] = s
            pen_a, pen_b = penalties(chunk)
            s_max[slot, 0:1, :] = jnp.maximum(
                jnp.max(s[:half], axis=0, keepdims=True) - pen_a, jnp.max(s[half:], axis=0, keepdims=True) - pen_b
            )

        def weigh(i, slot):
            pair, chunk = place(i)
            pen_a, pen_b = penalties(chunk)
            if base == 0:
                new = s_max[slot, 0:1, :]
            else:
                old = run_max[pair, 0:1, :]
                new = jnp.maximum(old, s_max[slot, 0:1, :])
                fade = jnp.exp2((old - new) * SCALE)
            run_max[pair, 0:1, :] = new
            s = s_buf[slot]
            weights = jnp.concatenate(
                [
                    jnp.exp2(((s[:half] - (new + pen_a)) * SCALE).astype(BF)),
                    jnp.exp2(((s[half:] - (new + pen_b)) * SCALE).astype(BF)),
                ],
                axis=0,
            )
            at = pl.multiple_of(chunk * CHUNK, CHUNK)
            for b in range(2):
                h = 2 * pair + b
                cols = slice(b * TOK, (b + 1) * TOK)
                part = dot(vaug[h, :, pl.ds(at, CHUNK)], weights[:, cols])
                if base:
                    part = acc[h] * fade[:, cols] + part
                acc[h] = part

        pipeline(5 * chunks, scores, weigh)

    window(own, 0)
    attend_window(0, 1)
    halo_here(0)
    window(halo_lr[0].reshape(CHUNK, C), 1)
    attend_window(1, 1)

    each(1, 16, lambda k: exchanged(k).wait_recv())
    for i in range(2):
        ring(i).start()
    across(0).start()
    halo_start(1)
    for i in (2, 3):
        halo_here(i)
    for i in range(4, 8):
        halo_start(i)
    window(halo_s[:2].reshape(CHUNK, C), 2)
    for i in (4, 5):
        halo_here(i)
    window(halo_s[2:4].reshape(CHUNK, C), 3)
    attend_window(2, 2)

    wkd[:, :256] = wk_ref[:, pl.ds(pl.multiple_of(core * 384, 128), 256)]
    wkd[:, 256:] = wk_ref[:, 256:384]
    wqd[:256] = wqt[pl.ds(pl.multiple_of(core * 384, 128), 256), :]
    wqd[256:] = wqt[pl.ds(pl.multiple_of(256 + core * 64, 64), HD), :]
    wvd[:256] = wvt[pl.ds(pl.multiple_of(core * 384, 128), 256), :]
    wvd[256:] = wvt[pl.ds(pl.multiple_of(256 + core * 64, 64), HD), :]
    qd[...] = jnp.zeros_like(qd)
    max_d[...] = jnp.full_like(max_d, NEG)
    acc_d[...] = jnp.zeros_like(acc_d)

    crossed(0).wait_recv()
    for c in range(2):
        tokens = gat[z, c].reshape(CHUNK, C)
        part = dot_nt(wqd[...], tokens).astype(BF)
        cols = slice(c * CHUNK, (c + 1) * CHUNK)
        for i in range(4):
            qd[i, i % 2 * HD : i % 2 * HD + HD, cols] = part[i * HD : (i + 1) * HD]
        qd[4, pl.ds(pl.multiple_of(core * HD, HD), HD), cols] = part[256:]

    def sub_chunk(g):
        plane = jnp.where(g < 2, 0, jnp.where(g > 5, 2, jnp.where(g % 2 == 0, 3, 1)))
        own_core = (g == 0) | (g == 2) | (g == 3) | (g == 6)
        tokens = gat[(z + plane) % 4, jnp.where(own_core, core, 1 - core)].reshape(CHUNK, C)
        at = pl.multiple_of(g * CHUNK, CHUNK)
        keys = dot(tokens, wkd[...]).astype(BF)
        for j in range(3):
            kd[j, pl.ds(at, CHUNK), :] = keys[:, j * 128 : (j + 1) * 128]
        vaug_d[:, :HD, pl.ds(at, CHUNK)] = dot_nt(wvd[...], tokens).astype(BF).reshape(5, HD, CHUNK)

    def give(j, k):
        s, c = (me + k // 2) % 16, (core + k) % 2
        return remote(
            dil.at[j, c * 16 + s], ret.at[core, j, me], r_send.at[j, k], r_recv.at[j, k], column(s, c)
        )

    def given(j, k):
        s, c = (me + 16 - k // 2) % 16, (core + k) % 2
        return remote(dil.at[j, 0], ret.at[c, j, s], r_send.at[j, k], r_recv.at[j, k], column(me, core))

    def attend_sub(first, heads, base, chunks):
        def place(i):
            return first + i // chunks, base + i % chunks

        def scores(i, slot):
            h, g = place(i)
            s = dot(kd[h // 2, pl.ds(pl.multiple_of(g * CHUNK, CHUNK), CHUNK), :], qd[h])
            s_buf[slot] = s
            s_max[slot, 0:1, :] = jnp.max(s, axis=0, keepdims=True)

        def weigh(i, slot):
            h, g = place(i)
            old = max_d[h, 0:1, :]
            new = jnp.maximum(old, s_max[slot, 0:1, :])
            fade = jnp.exp2((old - new) * SCALE)
            max_d[h, 0:1, :] = new
            weights = jnp.exp2(((s_buf[slot] - new) * SCALE).astype(BF))
            values = vaug_d[h, :, pl.ds(pl.multiple_of(g * CHUNK, CHUNK), CHUNK)]
            for b in range(2):
                cols = slice(b * TOK, (b + 1) * TOK)
                acc_d[h, :, cols] = acc_d[h, :, cols] * fade[:, cols] + dot(values, weights[:, cols])

        pipeline(chunks * heads, scores, weigh)

    each(0, 2, sub_chunk)
    attend_sub(0, 5, 0, 2)

    for i in (0, 1):
        ringed(i).wait_recv()
        ring(2 + i).start()
        across(1 + i).start()
    each(2, 4, sub_chunk)
    attend_sub(0, 5, 2, 2)

    for i in (1, 2):
        crossed(i).wait_recv()
    each(4, 6, sub_chunk)
    for i in (2, 3):
        ringed(i).wait_recv()
    across(3).start()
    sub_chunk(6)
    crossed(3).wait_recv()
    sub_chunk(7)
    for j in range(3):
        attend_sub(2 * j, 2 if j < 2 else 1, 4, 4)
        if j < 2:
            both = [acc_d[2 * j + b, :HD] / acc_d[2 * j + b, HD : HD + 1] for b in range(2)]
        else:
            only = acc_d[4, :HD] / acc_d[4, HD : HD + 1]
            both = [jnp.where(core == b, only, 0.0) for b in range(2)]
        dil[j] = jnp.concatenate(both, axis=0).T.astype(BF).reshape(32, 32, 128)
        each(1, 32, lambda k: give(j, k).start())
        ret[core, j, me] = dil[j, core * 16 + me]

    halo_here(1)
    window(halo_lr[1].reshape(CHUNK, C), 4)
    for i in (6, 7):
        halo_here(i)
    window(halo_s[4:].reshape(CHUNK, C), 5)
    attend_window(4, 2)
    for j in range(5):
        both = [acc[2 * j + b, :HD] / acc[2 * j + b, HD : HD + 1] for b in range(2)]
        local[:, j * 128 : (j + 1) * 128] = jnp.concatenate(both, axis=0).T

    def position(ref, natural_of):
        cols = jnp.where(
            natural_of((TOK, 16), 0) % 16 == lax.broadcasted_iota(jnp.int32, (TOK, 16), 1), 1.0, 0.0
        )
        spread = jnp.dot(cols, ref[...], preferred_element_type=F32, precision=lax.Precision.HIGHEST)
        here = natural_of((TOK, 32), 0) // 16 == lax.broadcasted_iota(jnp.int32, (TOK, 32), 1)
        return jnp.sum(jnp.where(here, spread, 0.0), axis=1, keepdims=True)

    def plain(shape, dim):
        return lax.broadcasted_iota(jnp.int32, shape, dim)

    mixing = position(blend_ref, order)
    keeping = position(skip_ref, plain)
    token = plain((TOK, 128), 0)
    source = token // 32 * 8 + token % 16 // 2
    repeat = jnp.where(source == lax.broadcasted_iota(jnp.int32, (TOK, 128), 1), 1.0, 0.0).astype(BF)
    upsampled = dot(repeat, previous_ref[...])
    place_back = jnp.where(
        order((TOK, TOK), 1) == lax.broadcasted_iota(jnp.int32, (TOK, TOK), 0), 1.0, 0.0
    ).astype(BF)

    for j in range(3):
        each(1, 32, lambda k: given(j, k).wait_recv())

    columns = []
    for pair in range(5):
        if pair == 2:
            dilated = ret[0, 2].astype(F32) + ret[1, 2].astype(F32)
        else:
            dilated = ret[pair // 3, pair % 3].astype(F32)
        dilated = dilated.reshape(TOK, 128)
        columns.append(
            ((1.0 - mixing) * local[:, pair * 128 : (pair + 1) * 128] + mixing * dilated).astype(BF)
        )
    mixed = dot(place_back, jnp.concatenate(columns, axis=1)).astype(BF)
    attention = dot(mixed, wo_ref[...])
    out_ref[...] = (
        (1.0 - keeping) * (latent_ref[...].astype(F32) + attention) + keeping * upsampled
    ).astype(BF)

    each(1, 16, lambda k: exchange(k).wait_send())
    for i in range(8):
        halo_sent(i)
    for i in range(4):
        ring(i).wait_send()
        across(i).wait_send()
    for j in range(3):
        each(1, 32, lambda k: give(j, k).wait_send())


def shards(latent, previous, blend_weight, skip_weight, norm_gain, w_query, w_key, w_value, w_out):
    vmem = pltpu.VMEM
    dma = pltpu.SemaphoreType.DMA
    result = pl.pallas_call(
        kernel,
        out_shape=jax.ShapeDtypeStruct((TOK, C), BF),
        in_specs=[pl.BlockSpec(memory_space=pltpu.VMEM)] * 9,
        out_specs=pl.BlockSpec(memory_space=pltpu.VMEM),
        scratch_shapes=[
            vmem((C, C), BF),
            vmem((C, C), BF),
            vmem((16, 32, C), BF),
            vmem((2, 16, 32, C), BF),
            vmem((6, 16, 16, C), BF),
            vmem((4, 2, 16, 32, C), BF),
            vmem((5, 128, ROWS), BF),
            vmem((WIN, C), BF),
            vmem((HEADS, AUG, WIN), BF),
            vmem((HEADS, AUG, TOK), F32),
            vmem((5, 8, ROWS), F32),
            vmem((2, CHUNK, ROWS), F32),
            vmem((2, 8, ROWS), F32),
            vmem((C, 384), BF),
            vmem((320, C), BF),
            vmem((320, C), BF),
            vmem((5, 128, ROWS), BF),
            vmem((3, SUB, 128), BF),
            vmem((5, AUG, SUB), BF),
            vmem((5, AUG, ROWS), F32),
            vmem((5, 8, ROWS), F32),
            vmem((3, 32, 32, 128), BF),
            vmem((2, 3, 16, 32, 128), BF),
            vmem((TOK, C), F32),
            dma((16,)), dma((16,)), dma((8,)), dma((8,)), dma((4,)), dma((4,)), dma((4,)), dma((4,)),
            dma((3, 32)), dma((3, 32)),
        ],
        compiler_params=pltpu.CompilerParams(
            collective_id=0, has_side_effects=True, vmem_limit_bytes=60 * 2**20
        ),
    )(
        latent.reshape(TOK, C), previous.reshape(128, C), blend_weight.T, skip_weight.T,
        norm_gain, w_query, w_key, w_value, w_out,
    )
    return result.reshape(latent.shape)


def solution(mesh):
    return jax.shard_map(
        shards,
        mesh=mesh,
        in_specs=(
            P(None, "tile", "phase", None),
            P(None, "tile", "phase", None),
            P("tile", "phase"),
            P("tile", "phase"),
            P(),
            P(),
            P(),
            P(),
            P(),
        ),
        out_specs=P(None, "tile", "phase", None),
        check_vma=False,
    )
```

```python
import functools

import jax
import jax.numpy as jnp
from jax import lax
from jax.experimental import pallas as pl
from jax.experimental.pallas import tpu as pltpu
from jax.sharding import PartitionSpec as P

HEADS = 10
HD = 64
C = 640
TOK = 512
CHUNK = 512
WIN = 3072
SUB = 4096
ROWS = 1024
AUG = 80
NEG = -1e30
SCALE = 0.125 * 1.4426950408889634
MESH = pl.DeviceIdType.MESH
BF = jnp.bfloat16
F32 = jnp.float32


def dot(a, b):
    return jnp.dot(a, b, preferred_element_type=F32)


def dot_nt(a, b):
    return lax.dot_general(a, b, (((1,), (1,)), ((), ())), preferred_element_type=F32)


def pipeline(count, scores, weigh):
    scores(0, 0)
    loops = (count - 1) // 2

    def body(i, carry):
        scores(2 * i + 1, 1)
        weigh(2 * i, 0)
        scores(2 * i + 2, 0)
        weigh(2 * i + 1, 1)
        return carry

    if loops:
        lax.fori_loop(0, loops, body, 0)
    if count % 2:
        weigh(count - 1, 0)
    else:
        scores(count - 1, 1)
        weigh(count - 2, 0)
        weigh(count - 1, 1)


def kernel(
    latent_ref, previous_ref, blend_ref, skip_ref, gain_ref, wq_ref, wk_ref, wv_ref, wo_ref,
    out_ref,
    wqt, wvt, nrm, halo_lr, halo_s, gat, qpad, kwin, vaug, acc, run_max, s_buf, s_max,
    wkd, wqd, wvd, qd, kd, vaug_d, acc_d, max_d, dil, ret, local,
    a2a_send, a2a_recv, halo_send, halo_recv, z_send, z_recv, c_send, c_recv, r_send, r_recv,
):
    t, p = lax.axis_index("tile"), lax.axis_index("phase")
    z, y_hi = t % 4, t // 4
    x, y_lo, core = p // 4, (p // 2) % 2, p % 2
    me = x * 4 + y_hi * 2 + y_lo

    def column(s, c):
        return ((s // 2) % 2 * 4 + z, s // 4 * 4 + s % 2 * 2 + c)

    up, down = ((t + 7) % 8, p), ((t + 1) % 8, p)
    far = (t, (p + 15 + 2 * core) % 16)
    z_next, z_prev = (y_hi * 4 + (z + 1) % 4, p), (y_hi * 4 + (z + 3) % 4, p)
    other = (t, p + 1 - 2 * core)

    barrier = pltpu.get_barrier_semaphore()
    for device in (up, down, far, z_next, z_prev):
        pl.semaphore_signal(barrier, inc=1, device_id=device, device_id_type=MESH)

    def greet(k, carry):
        pl.semaphore_signal(
            barrier, inc=1, device_id=column((me + k // 2) % 16, (core + k) % 2), device_id_type=MESH
        )
        return carry

    lax.fori_loop(1, 32, greet, 0)

    def order(shape, dim):
        r = lax.broadcasted_iota(jnp.int32, shape, dim)
        f, k = r // 32, r % 32
        return (4 * (k // 4) + f // 4) * 16 + 4 * (k % 4) + f % 4

    wide = latent_ref[...].astype(F32)
    average = jnp.mean(wide, axis=-1, keepdims=True)
    centred = wide - average
    variance = jnp.mean(centred * centred, axis=-1, keepdims=True)
    natural = (centred * lax.rsqrt(variance + 1e-5) * gain_ref[...][None, :]).astype(BF)
    pick = jnp.where(
        order((TOK, TOK), 0) == lax.broadcasted_iota(jnp.int32, (TOK, TOK), 1), 1.0, 0.0
    ).astype(BF)
    nrm[...] = dot(pick, natural).astype(BF).reshape(16, 32, C)

    pl.semaphore_wait(barrier, 36)

    def remote(src, dst, send, recv, device):
        return pltpu.make_async_remote_copy(
            src_ref=src, dst_ref=dst, send_sem=send, recv_sem=recv, device_id=device, device_id_type=MESH
        )

    def halo(i):
        if i < 2:
            return remote(nrm, halo_lr.at[i], halo_send.at[i], halo_recv.at[i], (other, far)[i])
        if i == 2:
            src, device = nrm.at[:, pl.ds(16, 16)], down
        elif i == 3:
            src, device = nrm.at[:, pl.ds(0, 16)], up
        else:
            src, device = halo_s.at[i % 2], (other, far)[(i - 4) // 2]
        return remote(src, halo_s.at[i - 2], halo_send.at[i], halo_recv.at[i], device)

    edge = ((core == 0) & (p == 0)) | ((core == 1) & (p == 15))
    above, below, beside = t > 0, t < 7, jnp.logical_not(edge)
    sends = (None, beside, below, above, above, below, above & beside, below & beside)
    receives = (None, beside, above, below, above, below, above & beside, below & beside)

    def when(condition, act):
        if condition is None:
            act()
        else:
            pl.when(condition)(act)

    def halo_start(i):
        when(sends[i], lambda: halo(i).start())

    def halo_sent(i):
        when(sends[i], lambda: halo(i).wait_send())

    def halo_here(i):
        when(receives[i], lambda: halo(i).wait_recv())
        if receives[i] is not None:

            @pl.when(jnp.logical_not(receives[i]))
            def _():
                if i < 2:
                    halo_lr[i] = jnp.zeros((16, 32, C), BF)
                else:
                    halo_s[i - 2] = jnp.zeros((16, 16, C), BF)

    def exchange(k):
        to = (me + k) % 16
        return remote(
            nrm.at[to], gat.at[z, core, me], a2a_send.at[k], a2a_recv.at[k], column(to, core)
        )

    def exchanged(k):
        return remote(
            nrm.at[0], gat.at[z, core, (me + 16 - k) % 16], a2a_send.at[k], a2a_recv.at[k], column(me, core)
        )

    def ring(i):
        if i < 2:
            shard = gat.at[z, core]
        else:
            shard = gat.at[(z + (3, 1)[i - 2]) % 4, core, pl.ds(8 * (i - 2), 8)]
        return remote(shard, shard, z_send.at[i], z_recv.at[i], (z_next, z_prev)[i % 2])

    def ringed(i):
        if i < 2:
            shard = gat.at[(z + (3, 1)[i]) % 4, core]
        else:
            shard = gat.at[(z + 2) % 4, core, pl.ds(8 * (i - 2), 8)]
        return remote(shard, shard, z_send.at[i], z_recv.at[i], (z_next, z_prev)[i % 2])

    def across(i):
        shard = gat.at[(z + (0, 3, 1, 2)[i]) % 4, core]
        return remote(shard, shard, c_send.at[i], c_recv.at[i], other)

    def crossed(i):
        shard = gat.at[(z + (0, 3, 1, 2)[i]) % 4, 1 - core]
        return remote(shard, shard, c_send.at[i], c_recv.at[i], other)

    def each(first, last, act):
        def body(k, carry):
            act(k)
            return carry

        lax.fori_loop(first, last, body, 0)

    halo_start(2)
    halo_start(3)
    each(1, 16, lambda k: exchange(k).start())
    halo_start(0)
    gat[z, core, me] = nrm[me]

    wqt[...] = wq_ref[...].T
    wvt[...] = wv_ref[...].T
    vaug[:, HD:, :] = jnp.ones((HEADS, AUG - HD, WIN), BF)
    vaug_d[:, HD:, :] = jnp.ones((5, AUG - HD, SUB), BF)

    own = nrm[...].reshape(TOK, C)
    queries = dot_nt(wqt[...], own).astype(BF)
    zeros = jnp.zeros((HD, TOK), BF)
    for j in range(5):
        first, second = queries[j * 128 : j * 128 + HD], queries[j * 128 + HD : j * 128 + 128]
        qpad[j, :HD, :TOK] = first
        qpad[j, HD:, :TOK] = zeros
        qpad[j, :HD, TOK:] = zeros
        qpad[j, HD:, TOK:] = second

    def window(tokens, chunk):
        at = pl.multiple_of(chunk * CHUNK, CHUNK)
        kwin[pl.ds(at, CHUNK), :] = dot(tokens, wk_ref[...]).astype(BF)
        vaug[:, :HD, pl.ds(at, CHUNK)] = dot_nt(wvt[...], tokens).astype(BF).reshape(HEADS, HD, CHUNK)

    top, bottom = t == 0, t == 7

    def penalties(chunk):
        corner = (chunk == 2) | (chunk == 3) | (chunk == 5)
        beyond = edge & (chunk >= 4)
        return (
            jnp.where((top & corner) | beyond, -NEG, 0.0),
            jnp.where((bottom & corner) | beyond, -NEG, 0.0),
        )

    half = CHUNK // 2

    def attend_window(base, chunks):
        def place(i):
            return i // chunks, base + i % chunks

        def scores(i, slot):
            pair, chunk = place(i)
            s = dot(
                kwin[pl.ds(pl.multiple_of(chunk * CHUNK, CHUNK), CHUNK), pl.ds(pl.multiple_of(pair * 128, 128), 128)],
                qpad[pair],
            )
            s_buf[slot] = s
            pen_a, pen_b = penalties(chunk)
            s_max[slot, 0:1, :] = jnp.maximum(
                jnp.max(s[:half], axis=0, keepdims=True) - pen_a, jnp.max(s[half:], axis=0, keepdims=True) - pen_b
            )

        def weigh(i, slot):
            pair, chunk = place(i)
            pen_a, pen_b = penalties(chunk)
            if base == 0:
                new = s_max[slot, 0:1, :]
            else:
                old = run_max[pair, 0:1, :]
                new = jnp.maximum(old, s_max[slot, 0:1, :])
                fade = jnp.exp2((old - new) * SCALE)
            run_max[pair, 0:1, :] = new
            s = s_buf[slot]
            weights = jnp.concatenate(
                [
                    jnp.exp2(((s[:half] - (new + pen_a)) * SCALE).astype(BF)),
                    jnp.exp2(((s[half:] - (new + pen_b)) * SCALE).astype(BF)),
                ],
                axis=0,
            )
            at = pl.multiple_of(chunk * CHUNK, CHUNK)
            for b in range(2):
                h = 2 * pair + b
                cols = slice(b * TOK, (b + 1) * TOK)
                part = dot(vaug[h, :, pl.ds(at, CHUNK)], weights[:, cols])
                if base:
                    part = acc[h] * fade[:, cols] + part
                acc[h] = part

        pipeline(5 * chunks, scores, weigh)

    window(own, 0)
    attend_window(0, 1)
    halo_here(0)
    window(halo_lr[0].reshape(CHUNK, C), 1)
    attend_window(1, 1)

    each(1, 16, lambda k: exchanged(k).wait_recv())
    for i in range(2):
        ring(i).start()
    across(0).start()

    wkd[:, :256] = wk_ref[:, pl.ds(pl.multiple_of(core * 384, 128), 256)]
    wkd[:, 256:] = wk_ref[:, 256:384]
    wqd[:256] = wqt[pl.ds(pl.multiple_of(core * 384, 128), 256), :]
    wqd[256:] = wqt[pl.ds(pl.multiple_of(256 + core * 64, 64), HD), :]
    wvd[:256] = wvt[pl.ds(pl.multiple_of(core * 384, 128), 256), :]
    wvd[256:] = wvt[pl.ds(pl.multiple_of(256 + core * 64, 64), HD), :]
    qd[...] = jnp.zeros_like(qd)
    max_d[...] = jnp.full_like(max_d, NEG)
    acc_d[...] = jnp.zeros_like(acc_d)

    def sub_chunk(g):
        plane = jnp.where(g < 2, 0, jnp.where(g > 5, 2, jnp.where(g % 2 == 0, 3, 1)))
        own_core = (g == 0) | (g == 2) | (g == 3) | (g == 6)
        tokens = gat[(z + plane) % 4, jnp.where(own_core, core, 1 - core)].reshape(CHUNK, C)
        at = pl.multiple_of(g * CHUNK, CHUNK)
        keys = dot(tokens, wkd[...]).astype(BF)
        for j in range(3):
            kd[j, pl.ds(at, CHUNK), :] = keys[:, j * 128 : (j + 1) * 128]
        vaug_d[:, :HD, pl.ds(at, CHUNK)] = dot_nt(wvd[...], tokens).astype(BF).reshape(5, HD, CHUNK)

    def give(j, k):
        s, c = (me + k // 2) % 16, (core + k) % 2
        return remote(
            dil.at[j, c * 16 + s], ret.at[core, j, me], r_send.at[j, k], r_recv.at[j, k], column(s, c)
        )

    def given(j, k):
        s, c = (me + 16 - k // 2) % 16, (core + k) % 2
        return remote(dil.at[j, 0], ret.at[c, j, s], r_send.at[j, k], r_recv.at[j, k], column(me, core))

    def attend_sub(first, heads, base, chunks):
        def place(i):
            return first + i // chunks, base + i % chunks

        def scores(i, slot):
            h, g = place(i)
            s = dot(kd[h // 2, pl.ds(pl.multiple_of(g * CHUNK, CHUNK), CHUNK), :], qd[h])
            s_buf[slot] = s
            s_max[slot, 0:1, :] = jnp.max(s, axis=0, keepdims=True)

        def weigh(i, slot):
            h, g = place(i)
            old = max_d[h, 0:1, :]
            new = jnp.maximum(old, s_max[slot, 0:1, :])
            fade = jnp.exp2((old - new) * SCALE)
            max_d[h, 0:1, :] = new
            weights = jnp.exp2(((s_buf[slot] - new) * SCALE).astype(BF))
            values = vaug_d[h, :, pl.ds(pl.multiple_of(g * CHUNK, CHUNK), CHUNK)]
            for b in range(2):
                cols = slice(b * TOK, (b + 1) * TOK)
                acc_d[h, :, cols] = acc_d[h, :, cols] * fade[:, cols] + dot(values, weights[:, cols])

        pipeline(chunks * heads, scores, weigh)

    def sub_queries(c):
        tokens = gat[z, c].reshape(CHUNK, C)
        part = dot_nt(wqd[...], tokens).astype(BF)
        cols = pl.ds(pl.multiple_of(c * CHUNK, CHUNK), CHUNK)
        for i in range(4):
            qd[i, i % 2 * HD : i % 2 * HD + HD, cols] = part[i * HD : (i + 1) * HD]
        qd[4, pl.ds(pl.multiple_of(core * HD, HD), HD), cols] = part[256:]

    sub_queries(core)
    sub_chunk(0)
    crossed(0).wait_recv()
    sub_queries(1 - core)
    sub_chunk(1)
    attend_sub(0, 5, 0, 2)

    for i in (2, 3):
        halo_here(i)
    for i in (4, 5):
        halo_start(i)
    halo_start(1)
    for i in (6, 7):
        halo_start(i)
    window(halo_s[:2].reshape(CHUNK, C), 2)
    for i in (4, 5):
        halo_here(i)
    window(halo_s[2:4].reshape(CHUNK, C), 3)
    attend_window(2, 2)

    for i in (0, 1):
        ringed(i).wait_recv()
        ring(2 + i).start()
        across(1 + i).start()
    each(2, 4, sub_chunk)
    attend_sub(0, 5, 2, 2)

    for i in (1, 2):
        crossed(i).wait_recv()
    each(4, 6, sub_chunk)
    for i in (2, 3):
        ringed(i).wait_recv()
    across(3).start()
    sub_chunk(6)
    crossed(3).wait_recv()
    sub_chunk(7)
    for j in range(3):
        attend_sub(2 * j, 2 if j < 2 else 1, 4, 4)
        if j < 2:
            both = [acc_d[2 * j + b, :HD] / acc_d[2 * j + b, HD : HD + 1] for b in range(2)]
        else:
            only = acc_d[4, :HD] / acc_d[4, HD : HD + 1]
            both = [jnp.where(core == b, only, 0.0) for b in range(2)]
        dil[j] = jnp.concatenate(both, axis=0).T.astype(BF).reshape(32, 32, 128)
        each(1, 32, lambda k: give(j, k).start())
        ret[core, j, me] = dil[j, core * 16 + me]

    halo_here(1)
    window(halo_lr[1].reshape(CHUNK, C), 4)
    for i in (6, 7):
        halo_here(i)
    window(halo_s[4:].reshape(CHUNK, C), 5)
    attend_window(4, 2)
    for j in range(5):
        both = [acc[2 * j + b, :HD] / acc[2 * j + b, HD : HD + 1] for b in range(2)]
        local[:, j * 128 : (j + 1) * 128] = jnp.concatenate(both, axis=0).T

    def position(ref, natural_of):
        cols = jnp.where(
            natural_of((TOK, 16), 0) % 16 == lax.broadcasted_iota(jnp.int32, (TOK, 16), 1), 1.0, 0.0
        )
        spread = jnp.dot(cols, ref[...], preferred_element_type=F32, precision=lax.Precision.HIGHEST)
        here = natural_of((TOK, 32), 0) // 16 == lax.broadcasted_iota(jnp.int32, (TOK, 32), 1)
        return jnp.sum(jnp.where(here, spread, 0.0), axis=1, keepdims=True)

    def plain(shape, dim):
        return lax.broadcasted_iota(jnp.int32, shape, dim)

    mixing = position(blend_ref, order)
    keeping = position(skip_ref, plain)
    token = plain((TOK, 128), 0)
    source = token // 32 * 8 + token % 16 // 2
    repeat = jnp.where(source == lax.broadcasted_iota(jnp.int32, (TOK, 128), 1), 1.0, 0.0).astype(BF)
    upsampled = dot(repeat, previous_ref[...])
    place_back = jnp.where(
        order((TOK, TOK), 1) == lax.broadcasted_iota(jnp.int32, (TOK, TOK), 0), 1.0, 0.0
    ).astype(BF)

    for j in range(3):
        each(1, 32, lambda k: given(j, k).wait_recv())

    columns = []
    for pair in range(5):
        if pair == 2:
            dilated = ret[0, 2].astype(F32) + ret[1, 2].astype(F32)
        else:
            dilated = ret[pair // 3, pair % 3].astype(F32)
        dilated = dilated.reshape(TOK, 128)
        columns.append(
            ((1.0 - mixing) * local[:, pair * 128 : (pair + 1) * 128] + mixing * dilated).astype(BF)
        )
    mixed = dot(place_back, jnp.concatenate(columns, axis=1)).astype(BF)
    attention = dot(mixed, wo_ref[...])
    out_ref[...] = (
        (1.0 - keeping) * (latent_ref[...].astype(F32) + attention) + keeping * upsampled
    ).astype(BF)

    each(1, 16, lambda k: exchange(k).wait_send())
    for i in range(8):
        halo_sent(i)
    for i in range(4):
        ring(i).wait_send()
        across(i).wait_send()
    for j in range(3):
        each(1, 32, lambda k: give(j, k).wait_send())


def shards(latent, previous, blend_weight, skip_weight, norm_gain, w_query, w_key, w_value, w_out):
    vmem = pltpu.VMEM
    dma = pltpu.SemaphoreType.DMA
    result = pl.pallas_call(
        kernel,
        out_shape=jax.ShapeDtypeStruct((TOK, C), BF),
        in_specs=[pl.BlockSpec(memory_space=pltpu.VMEM)] * 9,
        out_specs=pl.BlockSpec(memory_space=pltpu.VMEM),
        scratch_shapes=[
            vmem((C, C), BF),
            vmem((C, C), BF),
            vmem((16, 32, C), BF),
            vmem((2, 16, 32, C), BF),
            vmem((6, 16, 16, C), BF),
            vmem((4, 2, 16, 32, C), BF),
            vmem((5, 128, ROWS), BF),
            vmem((WIN, C), BF),
            vmem((HEADS, AUG, WIN), BF),
            vmem((HEADS, AUG, TOK), F32),
            vmem((5, 8, ROWS), F32),
            vmem((2, CHUNK, ROWS), F32),
            vmem((2, 8, ROWS), F32),
            vmem((C, 384), BF),
            vmem((320, C), BF),
            vmem((320, C), BF),
            vmem((5, 128, ROWS), BF),
            vmem((3, SUB, 128), BF),
            vmem((5, AUG, SUB), BF),
            vmem((5, AUG, ROWS), F32),
            vmem((5, 8, ROWS), F32),
            vmem((3, 32, 32, 128), BF),
            vmem((2, 3, 16, 32, 128), BF),
            vmem((TOK, C), F32),
            dma((16,)), dma((16,)), dma((8,)), dma((8,)), dma((4,)), dma((4,)), dma((4,)), dma((4,)),
            dma((3, 32)), dma((3, 32)),
        ],
        compiler_params=pltpu.CompilerParams(
            collective_id=0, has_side_effects=True, vmem_limit_bytes=60 * 2**20
        ),
    )(
        latent.reshape(TOK, C), previous.reshape(128, C), blend_weight.T, skip_weight.T,
        norm_gain, w_query, w_key, w_value, w_out,
    )
    return result.reshape(latent.shape)


def solution(mesh):
    return jax.shard_map(
        shards,
        mesh=mesh,
        in_specs=(
            P(None, "tile", "phase", None),
            P(None, "tile", "phase", None),
            P("tile", "phase"),
            P("tile", "phase"),
            P(),
            P(),
            P(),
            P(),
            P(),
        ),
        out_specs=P(None, "tile", "phase", None),
        check_vma=False,
    )
```

```python
import functools

import jax
import jax.numpy as jnp
from jax import lax
from jax.experimental import pallas as pl
from jax.experimental.pallas import tpu as pltpu
from jax.sharding import PartitionSpec as P

HEADS = 10
HD = 64
C = 640
TOK = 512
CHUNK = 512
WIN = 3072
SUB = 4096
ROWS = 1024
AUG = 80
NEG = -1e30
SCALE = 0.125 * 1.4426950408889634
MESH = pl.DeviceIdType.MESH
BF = jnp.bfloat16
F32 = jnp.float32


def dot(a, b):
    return jnp.dot(a, b, preferred_element_type=F32)


def dot_nt(a, b):
    return lax.dot_general(a, b, (((1,), (1,)), ((), ())), preferred_element_type=F32)


def pipeline(count, scores, weigh):
    scores(0, 0)
    loops = (count - 1) // 2

    def body(i, carry):
        scores(2 * i + 1, 1)
        weigh(2 * i, 0)
        scores(2 * i + 2, 0)
        weigh(2 * i + 1, 1)
        return carry

    if loops:
        lax.fori_loop(0, loops, body, 0)
    if count % 2:
        weigh(count - 1, 0)
    else:
        scores(count - 1, 1)
        weigh(count - 2, 0)
        weigh(count - 1, 1)


def kernel(
    latent_ref, previous_ref, blend_ref, skip_ref, gain_ref, wq_ref, wk_ref, wv_ref, wo_ref,
    out_ref,
    wqt, wvt, nrm, halo_lr, halo_s, gat, qpad, kwin, vaug, acc, run_max, s_buf, s_max,
    wkd, wqd, wvd, qd, kd, vaug_d, acc_d, max_d, dil, ret, local,
    a2a_send, a2a_recv, halo_send, halo_recv, z_send, z_recv, c_send, c_recv, r_send, r_recv,
):
    t, p = lax.axis_index("tile"), lax.axis_index("phase")
    z, y_hi = t % 4, t // 4
    x, y_lo, core = p // 4, (p // 2) % 2, p % 2
    me = x * 4 + y_hi * 2 + y_lo

    def column(s, c):
        return ((s // 2) % 2 * 4 + z, s // 4 * 4 + s % 2 * 2 + c)

    up, down = ((t + 7) % 8, p), ((t + 1) % 8, p)
    far = (t, (p + 15 + 2 * core) % 16)
    z_next, z_prev = (y_hi * 4 + (z + 1) % 4, p), (y_hi * 4 + (z + 3) % 4, p)
    other = (t, p + 1 - 2 * core)

    barrier = pltpu.get_barrier_semaphore()
    for device in (up, down, far, z_next, z_prev):
        pl.semaphore_signal(barrier, inc=1, device_id=device, device_id_type=MESH)

    def greet(k, carry):
        pl.semaphore_signal(
            barrier, inc=1, device_id=column((me + k // 2) % 16, (core + k) % 2), device_id_type=MESH
        )
        return carry

    lax.fori_loop(1, 32, greet, 0)

    def order(shape, dim):
        r = lax.broadcasted_iota(jnp.int32, shape, dim)
        f, k = r // 32, r % 32
        return (4 * (k // 4) + f // 4) * 16 + 4 * (k % 4) + f % 4

    wide = latent_ref[...].astype(F32)
    average = jnp.mean(wide, axis=-1, keepdims=True)
    centred = wide - average
    variance = jnp.mean(centred * centred, axis=-1, keepdims=True)
    natural = (centred * lax.rsqrt(variance + 1e-5) * gain_ref[...][None, :]).astype(BF)
    pick = jnp.where(
        order((TOK, TOK), 0) == lax.broadcasted_iota(jnp.int32, (TOK, TOK), 1), 1.0, 0.0
    ).astype(BF)
    nrm[...] = dot(pick, natural).astype(BF).reshape(16, 32, C)

    pl.semaphore_wait(barrier, 36)

    def remote(src, dst, send, recv, device):
        return pltpu.make_async_remote_copy(
            src_ref=src, dst_ref=dst, send_sem=send, recv_sem=recv, device_id=device, device_id_type=MESH
        )

    def halo(i):
        if i < 2:
            return remote(nrm, halo_lr.at[i], halo_send.at[i], halo_recv.at[i], (other, far)[i])
        if i == 2:
            src, device = nrm.at[:, pl.ds(16, 16)], down
        elif i == 3:
            src, device = nrm.at[:, pl.ds(0, 16)], up
        else:
            src, device = halo_s.at[i % 2], (other, far)[(i - 4) // 2]
        return remote(src, halo_s.at[i - 2], halo_send.at[i], halo_recv.at[i], device)

    edge = ((core == 0) & (p == 0)) | ((core == 1) & (p == 15))
    above, below, beside = t > 0, t < 7, jnp.logical_not(edge)
    sends = (None, beside, below, above, above, below, above & beside, below & beside)
    receives = (None, beside, above, below, above, below, above & beside, below & beside)

    def when(condition, act):
        if condition is None:
            act()
        else:
            pl.when(condition)(act)

    def halo_start(i):
        when(sends[i], lambda: halo(i).start())

    def halo_sent(i):
        when(sends[i], lambda: halo(i).wait_send())

    def halo_here(i):
        when(receives[i], lambda: halo(i).wait_recv())
        if receives[i] is not None:

            @pl.when(jnp.logical_not(receives[i]))
            def _():
                if i < 2:
                    halo_lr[i] = jnp.zeros((16, 32, C), BF)
                else:
                    halo_s[i - 2] = jnp.zeros((16, 16, C), BF)

    def exchange(k):
        to = (me + k) % 16
        return remote(
            nrm.at[to], gat.at[z, core, me], a2a_send.at[0], a2a_recv.at[0], column(to, core)
        )

    def exchanged():
        return remote(
            nrm.at[pl.ds(0, 15)], gat.at[z, core, pl.ds(0, 15)], a2a_send.at[0], a2a_recv.at[0], other
        )

    def ring(i):
        if i < 2:
            shard = gat.at[z, core]
        else:
            shard = gat.at[(z + (3, 1)[i - 2]) % 4, core, pl.ds(8 * (i - 2), 8)]
        return remote(shard, shard, z_send.at[i], z_recv.at[i], (z_next, z_prev)[i % 2])

    def ringed(i):
        if i < 2:
            shard = gat.at[(z + (3, 1)[i]) % 4, core]
        else:
            shard = gat.at[(z + 2) % 4, core, pl.ds(8 * (i - 2), 8)]
        return remote(shard, shard, z_send.at[i], z_recv.at[i], (z_next, z_prev)[i % 2])

    def across(i):
        shard = gat.at[(z + (0, 3, 1, 2)[i]) % 4, core]
        return remote(shard, shard, c_send.at[i], c_recv.at[i], other)

    def crossed(i):
        shard = gat.at[(z + (0, 3, 1, 2)[i]) % 4, 1 - core]
        return remote(shard, shard, c_send.at[i], c_recv.at[i], other)

    def each(first, last, act):
        def body(k, carry):
            act(k)
            return carry

        lax.fori_loop(first, last, body, 0)

    halo_start(2)
    halo_start(3)
    each(1, 16, lambda k: exchange(k).start())
    halo_start(0)
    gat[z, core, me] = nrm[me]

    wqt[...] = wq_ref[...].T
    wvt[...] = wv_ref[...].T
    vaug[:, HD:, :] = jnp.ones((HEADS, AUG - HD, WIN), BF)
    vaug_d[:, HD:, :] = jnp.ones((5, AUG - HD, SUB), BF)

    own = nrm[...].reshape(TOK, C)
    queries = dot_nt(wqt[...], own).astype(BF)
    zeros = jnp.zeros((HD, TOK), BF)
    for j in range(5):
        first, second = queries[j * 128 : j * 128 + HD], queries[j * 128 + HD : j * 128 + 128]
        qpad[j, :HD, :TOK] = first
        qpad[j, HD:, :TOK] = zeros
        qpad[j, :HD, TOK:] = zeros
        qpad[j, HD:, TOK:] = second

    def window(tokens, chunk):
        at = pl.multiple_of(chunk * CHUNK, CHUNK)
        kwin[pl.ds(at, CHUNK), :] = dot(tokens, wk_ref[...]).astype(BF)
        vaug[:, :HD, pl.ds(at, CHUNK)] = dot_nt(wvt[...], tokens).astype(BF).reshape(HEADS, HD, CHUNK)

    top, bottom = t == 0, t == 7

    def penalties(chunk):
        corner = (chunk == 2) | (chunk == 3) | (chunk == 5)
        beyond = edge & (chunk >= 4)
        return (
            jnp.where((top & corner) | beyond, -NEG, 0.0),
            jnp.where((bottom & corner) | beyond, -NEG, 0.0),
        )

    half = CHUNK // 2

    def attend_window(base, chunks):
        def place(i):
            return i // chunks, base + i % chunks

        def scores(i, slot):
            pair, chunk = place(i)
            s = dot(
                kwin[pl.ds(pl.multiple_of(chunk * CHUNK, CHUNK), CHUNK), pl.ds(pl.multiple_of(pair * 128, 128), 128)],
                qpad[pair],
            )
            s_buf[slot] = s
            pen_a, pen_b = penalties(chunk)
            s_max[slot, 0:1, :] = jnp.maximum(
                jnp.max(s[:half], axis=0, keepdims=True) - pen_a, jnp.max(s[half:], axis=0, keepdims=True) - pen_b
            )

        def weigh(i, slot):
            pair, chunk = place(i)
            pen_a, pen_b = penalties(chunk)
            if base == 0:
                new = s_max[slot, 0:1, :]
            else:
                old = run_max[pair, 0:1, :]
                new = jnp.maximum(old, s_max[slot, 0:1, :])
                fade = jnp.exp2((old - new) * SCALE)
            run_max[pair, 0:1, :] = new
            s = s_buf[slot]
            weights = jnp.concatenate(
                [
                    jnp.exp2(((s[:half] - (new + pen_a)) * SCALE).astype(BF)),
                    jnp.exp2(((s[half:] - (new + pen_b)) * SCALE).astype(BF)),
                ],
                axis=0,
            )
            at = pl.multiple_of(chunk * CHUNK, CHUNK)
            for b in range(2):
                h = 2 * pair + b
                cols = slice(b * TOK, (b + 1) * TOK)
                part = dot(vaug[h, :, pl.ds(at, CHUNK)], weights[:, cols])
                if base:
                    part = acc[h] * fade[:, cols] + part
                acc[h] = part

        pipeline(5 * chunks, scores, weigh)

    window(own, 0)
    attend_window(0, 1)
    halo_here(0)
    window(halo_lr[0].reshape(CHUNK, C), 1)
    attend_window(1, 1)

    exchanged().wait_recv()
    for i in range(2):
        ring(i).start()
    across(0).start()

    wkd[:, :256] = wk_ref[:, pl.ds(pl.multiple_of(core * 384, 128), 256)]
    wkd[:, 256:] = wk_ref[:, 256:384]
    wqd[:256] = wqt[pl.ds(pl.multiple_of(core * 384, 128), 256), :]
    wqd[256:] = wqt[pl.ds(pl.multiple_of(256 + core * 64, 64), HD), :]
    wvd[:256] = wvt[pl.ds(pl.multiple_of(core * 384, 128), 256), :]
    wvd[256:] = wvt[pl.ds(pl.multiple_of(256 + core * 64, 64), HD), :]
    qd[...] = jnp.zeros_like(qd)
    max_d[...] = jnp.full_like(max_d, NEG)
    acc_d[...] = jnp.zeros_like(acc_d)

    def sub_chunk(g):
        plane = jnp.where(g < 2, 0, jnp.where(g > 5, 2, jnp.where(g % 2 == 0, 3, 1)))
        own_core = (g == 0) | (g == 2) | (g == 3) | (g == 6)
        tokens = gat[(z + plane) % 4, jnp.where(own_core, core, 1 - core)].reshape(CHUNK, C)
        at = pl.multiple_of(g * CHUNK, CHUNK)
        keys = dot(tokens, wkd[...]).astype(BF)
        for j in range(3):
            kd[j, pl.ds(at, CHUNK), :] = keys[:, j * 128 : (j + 1) * 128]
        vaug_d[:, :HD, pl.ds(at, CHUNK)] = dot_nt(wvd[...], tokens).astype(BF).reshape(5, HD, CHUNK)

    def give(j, k):
        s, c = (me + k // 2) % 16, (core + k) % 2
        slots = (0, pl.ds(1, 2))[j]
        return remote(
            dil.at[slots, c * 16 + s], ret.at[core, slots, me], r_send.at[j], r_recv.at[j], column(s, c)
        )

    def given(j):
        part = dil.at[(0, pl.ds(1, 2))[j], pl.ds(0, 31)]
        return remote(part, part, r_send.at[j], r_recv.at[j], other)

    def attend_sub(first, heads, base, chunks):
        def place(i):
            return first + i // chunks, base + i % chunks

        def scores(i, slot):
            h, g = place(i)
            s = dot(kd[h // 2, pl.ds(pl.multiple_of(g * CHUNK, CHUNK), CHUNK), :], qd[h])
            s_buf[slot] = s
            s_max[slot, 0:1, :] = jnp.max(s, axis=0, keepdims=True)

        def weigh(i, slot):
            h, g = place(i)
            old = max_d[h, 0:1, :]
            new = jnp.maximum(old, s_max[slot, 0:1, :])
            fade = jnp.exp2((old - new) * SCALE)
            max_d[h, 0:1, :] = new
            weights = jnp.exp2(((s_buf[slot] - new) * SCALE).astype(BF))
            values = vaug_d[h, :, pl.ds(pl.multiple_of(g * CHUNK, CHUNK), CHUNK)]
            for b in range(2):
                cols = slice(b * TOK, (b + 1) * TOK)
                acc_d[h, :, cols] = acc_d[h, :, cols] * fade[:, cols] + dot(values, weights[:, cols])

        pipeline(chunks * heads, scores, weigh)

    def sub_queries(c):
        tokens = gat[z, c].reshape(CHUNK, C)
        part = dot_nt(wqd[...], tokens).astype(BF)
        cols = pl.ds(pl.multiple_of(c * CHUNK, CHUNK), CHUNK)
        for i in range(4):
            qd[i, i % 2 * HD : i % 2 * HD + HD, cols] = part[i * HD : (i + 1) * HD]
        qd[4, pl.ds(pl.multiple_of(core * HD, HD), HD), cols] = part[256:]

    sub_queries(core)
    sub_chunk(0)
    crossed(0).wait_recv()
    sub_queries(1 - core)
    sub_chunk(1)
    attend_sub(0, 5, 0, 2)

    for i in (2, 3):
        halo_here(i)
    for i in (4, 5):
        halo_start(i)
    halo_start(1)
    for i in (6, 7):
        halo_start(i)
    window(halo_s[:2].reshape(CHUNK, C), 2)
    attend_window(2, 1)
    for i in (4, 5):
        halo_here(i)
    window(halo_s[2:4].reshape(CHUNK, C), 3)
    attend_window(3, 1)

    for i in (0, 1):
        ringed(i).wait_recv()
        ring(2 + i).start()
        across(1 + i).start()
    each(2, 4, sub_chunk)
    attend_sub(0, 5, 2, 2)

    for i in (1, 2):
        crossed(i).wait_recv()
    each(4, 6, sub_chunk)
    for i in (2, 3):
        ringed(i).wait_recv()
    across(3).start()
    attend_sub(0, 5, 4, 2)
    crossed(3).wait_recv()
    each(6, 8, sub_chunk)
    for j in range(3):
        attend_sub(2 * j, 2 if j < 2 else 1, 6, 2)
        if j < 2:
            both = [acc_d[2 * j + b, :HD] / acc_d[2 * j + b, HD : HD + 1] for b in range(2)]
        else:
            only = acc_d[4, :HD] / acc_d[4, HD : HD + 1]
            both = [jnp.where(core == b, only, 0.0) for b in range(2)]
        dil[j] = jnp.concatenate(both, axis=0).T.astype(BF).reshape(32, 32, 128)
        if j != 1:
            each(1, 32, lambda k: give(j // 2, k).start())
        ret[core, j, me] = dil[j, core * 16 + me]

    halo_here(1)
    window(halo_lr[1].reshape(CHUNK, C), 4)
    for i in (6, 7):
        halo_here(i)
    window(halo_s[4:].reshape(CHUNK, C), 5)
    attend_window(4, 2)
    for j in range(5):
        both = [acc[2 * j + b, :HD] / acc[2 * j + b, HD : HD + 1] for b in range(2)]
        local[:, j * 128 : (j + 1) * 128] = jnp.concatenate(both, axis=0).T

    def position(ref, natural_of):
        cols = jnp.where(
            natural_of((TOK, 16), 0) % 16 == lax.broadcasted_iota(jnp.int32, (TOK, 16), 1), 1.0, 0.0
        )
        spread = jnp.dot(cols, ref[...], preferred_element_type=F32, precision=lax.Precision.HIGHEST)
        here = natural_of((TOK, 32), 0) // 16 == lax.broadcasted_iota(jnp.int32, (TOK, 32), 1)
        return jnp.sum(jnp.where(here, spread, 0.0), axis=1, keepdims=True)

    def plain(shape, dim):
        return lax.broadcasted_iota(jnp.int32, shape, dim)

    mixing = position(blend_ref, order)
    keeping = position(skip_ref, plain)
    token = plain((TOK, 128), 0)
    source = token // 32 * 8 + token % 16 // 2
    repeat = jnp.where(source == lax.broadcasted_iota(jnp.int32, (TOK, 128), 1), 1.0, 0.0).astype(BF)
    upsampled = dot(repeat, previous_ref[...])
    place_back = jnp.where(
        order((TOK, TOK), 1) == lax.broadcasted_iota(jnp.int32, (TOK, TOK), 0), 1.0, 0.0
    ).astype(BF)

    for j in range(2):
        given(j).wait_recv()

    columns = []
    for pair in range(5):
        if pair == 2:
            dilated = ret[0, 2].astype(F32) + ret[1, 2].astype(F32)
        else:
            dilated = ret[pair // 3, pair % 3].astype(F32)
        dilated = dilated.reshape(TOK, 128)
        columns.append(
            ((1.0 - mixing) * local[:, pair * 128 : (pair + 1) * 128] + mixing * dilated).astype(BF)
        )
    mixed = dot(place_back, jnp.concatenate(columns, axis=1)).astype(BF)
    attention = dot(mixed, wo_ref[...])
    out_ref[...] = (
        (1.0 - keeping) * (latent_ref[...].astype(F32) + attention) + keeping * upsampled
    ).astype(BF)

    exchanged().wait_send()
    for i in range(8):
        halo_sent(i)
    for i in range(4):
        ring(i).wait_send()
        across(i).wait_send()
    for j in range(2):
        given(j).wait_send()


def shards(latent, previous, blend_weight, skip_weight, norm_gain, w_query, w_key, w_value, w_out):
    vmem = pltpu.VMEM
    dma = pltpu.SemaphoreType.DMA
    result = pl.pallas_call(
        kernel,
        out_shape=jax.ShapeDtypeStruct((TOK, C), BF),
        in_specs=[pl.BlockSpec(memory_space=pltpu.VMEM)] * 9,
        out_specs=pl.BlockSpec(memory_space=pltpu.VMEM),
        scratch_shapes=[
            vmem((C, C), BF),
            vmem((C, C), BF),
            vmem((16, 32, C), BF),
            vmem((2, 16, 32, C), BF),
            vmem((6, 16, 16, C), BF),
            vmem((4, 2, 16, 32, C), BF),
            vmem((5, 128, ROWS), BF),
            vmem((WIN, C), BF),
            vmem((HEADS, AUG, WIN), BF),
            vmem((HEADS, AUG, TOK), F32),
            vmem((5, 8, ROWS), F32),
            vmem((2, CHUNK, ROWS), F32),
            vmem((2, 8, ROWS), F32),
            vmem((C, 384), BF),
            vmem((320, C), BF),
            vmem((320, C), BF),
            vmem((5, 128, ROWS), BF),
            vmem((3, SUB, 128), BF),
            vmem((5, AUG, SUB), BF),
            vmem((5, AUG, ROWS), F32),
            vmem((5, 8, ROWS), F32),
            vmem((3, 32, 32, 128), BF),
            vmem((2, 3, 16, 32, 128), BF),
            vmem((TOK, C), F32),
            dma((1,)), dma((1,)), dma((8,)), dma((8,)), dma((4,)), dma((4,)), dma((4,)), dma((4,)),
            dma((2,)), dma((2,)),
        ],
        compiler_params=pltpu.CompilerParams(
            collective_id=0, has_side_effects=True, vmem_limit_bytes=60 * 2**20
        ),
    )(
        latent.reshape(TOK, C), previous.reshape(128, C), blend_weight.T, skip_weight.T,
        norm_gain, w_query, w_key, w_value, w_out,
    )
    return result.reshape(latent.shape)


def solution(mesh):
    return jax.shard_map(
        shards,
        mesh=mesh,
        in_specs=(
            P(None, "tile", "phase", None),
            P(None, "tile", "phase", None),
            P("tile", "phase"),
            P("tile", "phase"),
            P(),
            P(),
            P(),
            P(),
            P(),
        ),
        out_specs=P(None, "tile", "phase", None),
        check_vma=False,
    )
```

```python
import functools

import jax
import jax.numpy as jnp
from jax import lax
from jax.experimental import pallas as pl
from jax.experimental.pallas import tpu as pltpu
from jax.sharding import PartitionSpec as P

HEADS = 10
HD = 64
C = 640
TOK = 512
CHUNK = 512
WIN = 3072
SUB = 4096
ROWS = 1024
AUG = 80
NEG = -1e30
SCALE = 0.125 * 1.4426950408889634
MESH = pl.DeviceIdType.MESH
BF = jnp.bfloat16
F32 = jnp.float32


def dot(a, b):
    return jnp.dot(a, b, preferred_element_type=F32)


def dot_nt(a, b):
    return lax.dot_general(a, b, (((1,), (1,)), ((), ())), preferred_element_type=F32)


def pipeline(count, scores, weigh):
    scores(0, 0)
    loops = (count - 1) // 2

    def body(i, carry):
        scores(2 * i + 1, 1)
        weigh(2 * i, 0)
        scores(2 * i + 2, 0)
        weigh(2 * i + 1, 1)
        return carry

    if loops:
        lax.fori_loop(0, loops, body, 0)
    if count % 2:
        weigh(count - 1, 0)
    else:
        scores(count - 1, 1)
        weigh(count - 2, 0)
        weigh(count - 1, 1)


def kernel(
    latent_ref, previous_ref, blend_ref, skip_ref, gain_ref, wq_ref, wk_ref, wv_ref, wo_ref,
    out_ref,
    wqt, wvt, nrm, halo_lr, halo_s, gat, qpad, kwin, vaug, acc, run_max, s_buf, s_max,
    wkd, wqd, wvd, qd, kd, vaug_d, acc_d, max_d, dil, ret, local,
    a2a_send, a2a_recv, halo_send, halo_recv, z_send, z_recv, c_send, c_recv, r_send, r_recv,
):
    t, p = lax.axis_index("tile"), lax.axis_index("phase")
    z, y_hi = t % 4, t // 4
    x, y_lo, core = p // 4, (p // 2) % 2, p % 2
    me = x * 4 + y_hi * 2 + y_lo

    def column(s, c):
        return ((s // 2) % 2 * 4 + z, s // 4 * 4 + s % 2 * 2 + c)

    up, down = ((t + 7) % 8, p), ((t + 1) % 8, p)
    far = (t, (p + 15 + 2 * core) % 16)
    z_next, z_prev = (y_hi * 4 + (z + 1) % 4, p), (y_hi * 4 + (z + 3) % 4, p)
    other = (t, p + 1 - 2 * core)

    barrier = pltpu.get_barrier_semaphore()
    for device in (up, down, far, z_next, z_prev):
        pl.semaphore_signal(barrier, inc=1, device_id=device, device_id_type=MESH)

    def greet(k, carry):
        pl.semaphore_signal(
            barrier, inc=1, device_id=column((me + k // 2) % 16, (core + k) % 2), device_id_type=MESH
        )
        return carry

    lax.fori_loop(1, 32, greet, 0)

    def order(shape, dim):
        r = lax.broadcasted_iota(jnp.int32, shape, dim)
        f, k = r // 32, r % 32
        return (4 * (k // 4) + f // 4) * 16 + 4 * (k % 4) + f % 4

    wide = latent_ref[...].astype(F32)
    average = jnp.mean(wide, axis=-1, keepdims=True)
    centred = wide - average
    variance = jnp.mean(centred * centred, axis=-1, keepdims=True)
    natural = (centred * lax.rsqrt(variance + 1e-5) * gain_ref[...][None, :]).astype(BF)
    pick = jnp.where(
        order((TOK, TOK), 0) == lax.broadcasted_iota(jnp.int32, (TOK, TOK), 1), 1.0, 0.0
    ).astype(BF)
    nrm[...] = dot(pick, natural).astype(BF).reshape(16, 32, C)

    pl.semaphore_wait(barrier, 36)

    def remote(src, dst, send, recv, device):
        return pltpu.make_async_remote_copy(
            src_ref=src, dst_ref=dst, send_sem=send, recv_sem=recv, device_id=device, device_id_type=MESH
        )

    def halo(i):
        if i < 2:
            return remote(nrm, halo_lr.at[i], halo_send.at[i], halo_recv.at[i], (other, far)[i])
        if i == 2:
            src, device = nrm.at[:, pl.ds(16, 16)], down
        elif i == 3:
            src, device = nrm.at[:, pl.ds(0, 16)], up
        else:
            src, device = halo_s.at[i % 2], (other, far)[(i - 4) // 2]
        return remote(src, halo_s.at[i - 2], halo_send.at[i], halo_recv.at[i], device)

    edge = ((core == 0) & (p == 0)) | ((core == 1) & (p == 15))
    above, below, beside = t > 0, t < 7, jnp.logical_not(edge)
    sends = (None, beside, below, above, above, below, above & beside, below & beside)
    receives = (None, beside, above, below, above, below, above & beside, below & beside)

    def when(condition, act):
        if condition is None:
            act()
        else:
            pl.when(condition)(act)

    def halo_start(i):
        when(sends[i], lambda: halo(i).start())

    def halo_sent(i):
        when(sends[i], lambda: halo(i).wait_send())

    def halo_here(i):
        when(receives[i], lambda: halo(i).wait_recv())
        if receives[i] is not None:

            @pl.when(jnp.logical_not(receives[i]))
            def _():
                if i < 2:
                    halo_lr[i] = jnp.zeros((16, 32, C), BF)
                else:
                    halo_s[i - 2] = jnp.zeros((16, 16, C), BF)

    def exchange(k):
        to = (me + k) % 16
        return remote(
            nrm.at[to], gat.at[z, core, me], a2a_send.at[0], a2a_recv.at[0], column(to, core)
        )

    def exchanged():
        return remote(
            nrm.at[pl.ds(0, 15)], gat.at[z, core, pl.ds(0, 15)], a2a_send.at[0], a2a_recv.at[0], other
        )

    def ring(i):
        if i < 2:
            shard = gat.at[z, core]
        else:
            shard = gat.at[(z + (3, 1)[i - 2]) % 4, core, pl.ds(8 * (i - 2), 8)]
        return remote(shard, shard, z_send.at[i], z_recv.at[i], (z_next, z_prev)[i % 2])

    def ringed(i):
        if i < 2:
            shard = gat.at[(z + (3, 1)[i]) % 4, core]
        else:
            shard = gat.at[(z + 2) % 4, core, pl.ds(8 * (i - 2), 8)]
        return remote(shard, shard, z_send.at[i], z_recv.at[i], (z_next, z_prev)[i % 2])

    def across(i):
        shard = gat.at[(z + (0, 3, 1, 2)[i]) % 4, core]
        return remote(shard, shard, c_send.at[i], c_recv.at[i], other)

    def crossed(i):
        shard = gat.at[(z + (0, 3, 1, 2)[i]) % 4, 1 - core]
        return remote(shard, shard, c_send.at[i], c_recv.at[i], other)

    def each(first, last, act):
        def body(k, carry):
            act(k)
            return carry

        lax.fori_loop(first, last, body, 0)

    halo_start(2)
    halo_start(3)
    each(1, 16, lambda k: exchange(k).start())
    halo_start(0)
    gat[z, core, me] = nrm[me]

    wqt[...] = wq_ref[...].T
    wvt[...] = wv_ref[...].T
    vaug[:, HD:, :] = jnp.ones((HEADS, AUG - HD, WIN), BF)
    vaug_d[:, HD:, :] = jnp.ones((5, AUG - HD, SUB), BF)

    own = nrm[...].reshape(TOK, C)
    queries = dot_nt(wqt[...], own).astype(BF)
    zeros = jnp.zeros((HD, TOK), BF)
    for j in range(5):
        first, second = queries[j * 128 : j * 128 + HD], queries[j * 128 + HD : j * 128 + 128]
        qpad[j, :HD, :TOK] = first
        qpad[j, HD:, :TOK] = zeros
        qpad[j, :HD, TOK:] = zeros
        qpad[j, HD:, TOK:] = second

    def window(tokens, chunk):
        at = pl.multiple_of(chunk * CHUNK, CHUNK)
        kwin[pl.ds(at, CHUNK), :] = dot(tokens, wk_ref[...]).astype(BF)
        vaug[:, :HD, pl.ds(at, CHUNK)] = dot_nt(wvt[...], tokens).astype(BF).reshape(HEADS, HD, CHUNK)

    top, bottom = t == 0, t == 7

    def penalties(chunk):
        corner = (chunk == 2) | (chunk == 3) | (chunk == 5)
        beyond = edge & (chunk >= 4)
        return (
            jnp.where((top & corner) | beyond, -NEG, 0.0),
            jnp.where((bottom & corner) | beyond, -NEG, 0.0),
        )

    half = CHUNK // 2

    def attend_window(base, chunks):
        def place(i):
            return i // chunks, base + i % chunks

        def scores(i, slot):
            pair, chunk = place(i)
            s = dot(
                kwin[pl.ds(pl.multiple_of(chunk * CHUNK, CHUNK), CHUNK), pl.ds(pl.multiple_of(pair * 128, 128), 128)],
                qpad[pair],
            )
            s_buf[slot] = s
            pen_a, pen_b = penalties(chunk)
            s_max[slot, 0:1, :] = jnp.maximum(
                jnp.max(s[:half], axis=0, keepdims=True) - pen_a, jnp.max(s[half:], axis=0, keepdims=True) - pen_b
            )

        def weigh(i, slot):
            pair, chunk = place(i)
            pen_a, pen_b = penalties(chunk)
            if base == 0:
                new = s_max[slot, 0:1, :]
            else:
                old = run_max[pair, 0:1, :]
                new = jnp.maximum(old, s_max[slot, 0:1, :])
                fade = jnp.exp2((old - new) * SCALE)
            run_max[pair, 0:1, :] = new
            s = s_buf[slot]
            weights = jnp.concatenate(
                [
                    jnp.exp2(((s[:half] - (new + pen_a)) * SCALE).astype(BF)),
                    jnp.exp2(((s[half:] - (new + pen_b)) * SCALE).astype(BF)),
                ],
                axis=0,
            )
            at = pl.multiple_of(chunk * CHUNK, CHUNK)
            for b in range(2):
                h = 2 * pair + b
                cols = slice(b * TOK, (b + 1) * TOK)
                part = dot(vaug[h, :, pl.ds(at, CHUNK)], weights[:, cols])
                if base:
                    part = acc[h] * fade[:, cols] + part
                acc[h] = part

        pipeline(5 * chunks, scores, weigh)

    window(own, 0)
    attend_window(0, 1)
    halo_here(0)
    window(halo_lr[0].reshape(CHUNK, C), 1)
    attend_window(1, 1)

    exchanged().wait_recv()
    for i in range(2):
        ring(i).start()
    across(0).start()

    wkd[:, :256] = wk_ref[:, pl.ds(pl.multiple_of(core * 384, 128), 256)]
    wkd[:, 256:] = wk_ref[:, 256:384]
    wqd[:256] = wqt[pl.ds(pl.multiple_of(core * 384, 128), 256), :]
    wqd[256:] = wqt[pl.ds(pl.multiple_of(256 + core * 64, 64), HD), :]
    wvd[:256] = wvt[pl.ds(pl.multiple_of(core * 384, 128), 256), :]
    wvd[256:] = wvt[pl.ds(pl.multiple_of(256 + core * 64, 64), HD), :]
    qd[...] = jnp.zeros_like(qd)
    max_d[...] = jnp.full_like(max_d, NEG)
    acc_d[...] = jnp.zeros_like(acc_d)

    def sub_chunk(g):
        plane = jnp.where(g < 2, 0, jnp.where(g > 5, 2, jnp.where(g % 2 == 0, 3, 1)))
        own_core = (g == 0) | (g == 2) | (g == 3) | (g == 6)
        tokens = gat[(z + plane) % 4, jnp.where(own_core, core, 1 - core)].reshape(CHUNK, C)
        at = pl.multiple_of(g * CHUNK, CHUNK)
        keys = dot(tokens, wkd[...]).astype(BF)
        for j in range(3):
            kd[j, pl.ds(at, CHUNK), :] = keys[:, j * 128 : (j + 1) * 128]
        vaug_d[:, :HD, pl.ds(at, CHUNK)] = dot_nt(wvd[...], tokens).astype(BF).reshape(5, HD, CHUNK)

    def give(j, k):
        s, c = (me + k // 2) % 16, (core + k) % 2
        return remote(
            dil.at[j, c * 16 + s], ret.at[core, j, me], r_send.at[j], r_recv.at[j], column(s, c)
        )

    def given(j):
        part = dil.at[j, pl.ds(0, 31)]
        return remote(part, part, r_send.at[j], r_recv.at[j], other)

    def attend_sub(first, heads, base, chunks):
        def place(i):
            return first + i // chunks, base + i % chunks

        def scores(i, slot):
            h, g = place(i)
            s = dot(kd[h // 2, pl.ds(pl.multiple_of(g * CHUNK, CHUNK), CHUNK), :], qd[h])
            s_buf[slot] = s
            s_max[slot, 0:1, :] = jnp.max(s, axis=0, keepdims=True)

        def weigh(i, slot):
            h, g = place(i)
            old = max_d[h, 0:1, :]
            new = jnp.maximum(old, s_max[slot, 0:1, :])
            fade = jnp.exp2((old - new) * SCALE)
            max_d[h, 0:1, :] = new
            weights = jnp.exp2(((s_buf[slot] - new) * SCALE).astype(BF))
            values = vaug_d[h, :, pl.ds(pl.multiple_of(g * CHUNK, CHUNK), CHUNK)]
            for b in range(2):
                cols = slice(b * TOK, (b + 1) * TOK)
                acc_d[h, :, cols] = acc_d[h, :, cols] * fade[:, cols] + dot(values, weights[:, cols])

        pipeline(chunks * heads, scores, weigh)

    def sub_queries(c):
        tokens = gat[z, c].reshape(CHUNK, C)
        part = dot_nt(wqd[...], tokens).astype(BF)
        cols = pl.ds(pl.multiple_of(c * CHUNK, CHUNK), CHUNK)
        for i in range(4):
            qd[i, i % 2 * HD : i % 2 * HD + HD, cols] = part[i * HD : (i + 1) * HD]
        qd[4, pl.ds(pl.multiple_of(core * HD, HD), HD), cols] = part[256:]

    sub_queries(core)
    sub_chunk(0)
    crossed(0).wait_recv()
    sub_queries(1 - core)
    sub_chunk(1)
    attend_sub(0, 5, 0, 2)

    for i in (2, 3):
        halo_here(i)
    for i in (4, 5):
        halo_start(i)
    halo_start(1)
    for i in (6, 7):
        halo_start(i)
    window(halo_s[:2].reshape(CHUNK, C), 2)
    for i in (4, 5):
        halo_here(i)
    window(halo_s[2:4].reshape(CHUNK, C), 3)
    attend_window(2, 2)

    for i in (0, 1):
        ringed(i).wait_recv()
        ring(2 + i).start()
        across(1 + i).start()
    each(2, 4, sub_chunk)
    for i in (1, 2):
        crossed(i).wait_recv()
    each(4, 6, sub_chunk)
    attend_sub(0, 5, 2, 4)

    for i in (2, 3):
        ringed(i).wait_recv()
    across(3).start()
    sub_chunk(6)
    crossed(3).wait_recv()
    sub_chunk(7)
    for j in range(3):
        attend_sub(2 * j, 2 if j < 2 else 1, 6, 2)
        if j < 2:
            both = [acc_d[2 * j + b, :HD] / acc_d[2 * j + b, HD : HD + 1] for b in range(2)]
        else:
            only = acc_d[4, :HD] / acc_d[4, HD : HD + 1]
            both = [jnp.where(core == b, only, 0.0) for b in range(2)]
        dil[j] = jnp.concatenate(both, axis=0).T.astype(BF).reshape(32, 32, 128)
        each(1, 32, lambda k: give(j, k).start())
        ret[core, j, me] = dil[j, core * 16 + me]

    halo_here(1)
    window(halo_lr[1].reshape(CHUNK, C), 4)
    for i in (6, 7):
        halo_here(i)
    window(halo_s[4:].reshape(CHUNK, C), 5)
    attend_window(4, 2)
    for j in range(5):
        both = [acc[2 * j + b, :HD] / acc[2 * j + b, HD : HD + 1] for b in range(2)]
        local[:, j * 128 : (j + 1) * 128] = jnp.concatenate(both, axis=0).T

    def position(ref, natural_of):
        cols = jnp.where(
            natural_of((TOK, 16), 0) % 16 == lax.broadcasted_iota(jnp.int32, (TOK, 16), 1), 1.0, 0.0
        )
        spread = jnp.dot(cols, ref[...], preferred_element_type=F32, precision=lax.Precision.HIGHEST)
        here = natural_of((TOK, 32), 0) // 16 == lax.broadcasted_iota(jnp.int32, (TOK, 32), 1)
        return jnp.sum(jnp.where(here, spread, 0.0), axis=1, keepdims=True)

    def plain(shape, dim):
        return lax.broadcasted_iota(jnp.int32, shape, dim)

    mixing = position(blend_ref, order)
    keeping = position(skip_ref, plain)
    token = plain((TOK, 128), 0)
    source = token // 32 * 8 + token % 16 // 2
    repeat = jnp.where(source == lax.broadcasted_iota(jnp.int32, (TOK, 128), 1), 1.0, 0.0).astype(BF)
    upsampled = dot(repeat, previous_ref[...])
    place_back = jnp.where(
        order((TOK, TOK), 1) == lax.broadcasted_iota(jnp.int32, (TOK, TOK), 0), 1.0, 0.0
    ).astype(BF)

    for j in range(3):
        given(j).wait_recv()

    columns = []
    for pair in range(5):
        if pair == 2:
            dilated = ret[0, 2].astype(F32) + ret[1, 2].astype(F32)
        else:
            dilated = ret[pair // 3, pair % 3].astype(F32)
        dilated = dilated.reshape(TOK, 128)
        columns.append(
            ((1.0 - mixing) * local[:, pair * 128 : (pair + 1) * 128] + mixing * dilated).astype(BF)
        )
    mixed = dot(place_back, jnp.concatenate(columns, axis=1)).astype(BF)
    attention = dot(mixed, wo_ref[...])
    out_ref[...] = (
        (1.0 - keeping) * (latent_ref[...].astype(F32) + attention) + keeping * upsampled
    ).astype(BF)

    exchanged().wait_send()
    for i in range(8):
        halo_sent(i)
    for i in range(4):
        ring(i).wait_send()
        across(i).wait_send()
    for j in range(3):
        given(j).wait_send()


def shards(latent, previous, blend_weight, skip_weight, norm_gain, w_query, w_key, w_value, w_out):
    vmem = pltpu.VMEM
    dma = pltpu.SemaphoreType.DMA
    result = pl.pallas_call(
        kernel,
        out_shape=jax.ShapeDtypeStruct((TOK, C), BF),
        in_specs=[pl.BlockSpec(memory_space=pltpu.VMEM)] * 9,
        out_specs=pl.BlockSpec(memory_space=pltpu.VMEM),
        scratch_shapes=[
            vmem((C, C), BF),
            vmem((C, C), BF),
            vmem((16, 32, C), BF),
            vmem((2, 16, 32, C), BF),
            vmem((6, 16, 16, C), BF),
            vmem((4, 2, 16, 32, C), BF),
            vmem((5, 128, ROWS), BF),
            vmem((WIN, C), BF),
            vmem((HEADS, AUG, WIN), BF),
            vmem((HEADS, AUG, TOK), F32),
            vmem((5, 8, ROWS), F32),
            vmem((2, CHUNK, ROWS), F32),
            vmem((2, 8, ROWS), F32),
            vmem((C, 384), BF),
            vmem((320, C), BF),
            vmem((320, C), BF),
            vmem((5, 128, ROWS), BF),
            vmem((3, SUB, 128), BF),
            vmem((5, AUG, SUB), BF),
            vmem((5, AUG, ROWS), F32),
            vmem((5, 8, ROWS), F32),
            vmem((3, 32, 32, 128), BF),
            vmem((2, 3, 16, 32, 128), BF),
            vmem((TOK, C), F32),
            dma((1,)), dma((1,)), dma((8,)), dma((8,)), dma((4,)), dma((4,)), dma((4,)), dma((4,)),
            dma((3,)), dma((3,)),
        ],
        compiler_params=pltpu.CompilerParams(
            collective_id=0, has_side_effects=True, vmem_limit_bytes=60 * 2**20
        ),
    )(
        latent.reshape(TOK, C), previous.reshape(128, C), blend_weight.T, skip_weight.T,
        norm_gain, w_query, w_key, w_value, w_out,
    )
    return result.reshape(latent.shape)


def solution(mesh):
    return jax.shard_map(
        shards,
        mesh=mesh,
        in_specs=(
            P(None, "tile", "phase", None),
            P(None, "tile", "phase", None),
            P("tile", "phase"),
            P("tile", "phase"),
            P(),
            P(),
            P(),
            P(),
            P(),
        ),
        out_specs=P(None, "tile", "phase", None),
        check_vma=False,
    )
```
